128 devices in a mesh: occ: 32 (over x, y_lo, z), aux: 4 (over y_hi, core).
Axes of the slice: x: 4, y: 4 (y_hi: 2, y_lo: 2; y = y_hi * 2 + y_lo), z: 4, core: 2. Of those that a mesh axis runs over, the one named last changes fastest.
Arguments:
- b_aux: bfloat16 [8192, 64, 256], P(('occ', 'aux')), may hold values from -0.06982422 to 0.06982422
- eps_occ: float32 [64], replicated, may hold values from -3 to -0.3
- eps_vir: float32 [4096], replicated, may hold values from 0.5 to 3
- domains: int32 [64, 2], replicated, may hold values from 0 to 31
- pair_keep: int32 [64, 7], P('occ'), may hold values 0 or 1
Outputs:
- gamma: bfloat16 [8192, 64, 256], P(('occ', 'aux'))
The draws below stay inside these ranges and needn't reach their ends.
All inputs are finite; a program needn't handle non-finite values. No bound on the sum of `pair_keep` on one device may be relied on, other than what follows from the above.
Results may differ from the reference program's by a relative error of at most 0.0042.
Values may be sent and summed in bfloat16 or wider, within the bound.
A program may use at most 128 MiB of HBM per device.

```python
import jax
import jax.numpy as jnp
from jax import lax

NAUX = 8192
NVIR = 4096
VBLK = 128
KMAX = 2
OCC_DEV = 2
H = 3
KW = 256
NOCC = 64
N_OCC = 32


def plant(result, own_key, low, high):
    index_at = [jax.random.randint(jax.random.fold_in(own_key, axis), (), 0, length) for axis, length in enumerate(result.shape)]
    main_axis = result.shape.index(max(result.shape))
    beside = index_at[:main_axis] + [(index_at[main_axis] + 1) % result.shape[main_axis]] + index_at[main_axis + 1:]
    return result.at[tuple(index_at)].set(low).at[tuple(beside)].set(high)


def shard_levels(key, dims, shards, low, high):
    def one(dim, shards_of):
        steps = jax.random.uniform(jax.random.fold_in(jax.random.fold_in(key, 6), dim), (shards_of,), jnp.float32, low / len(shards), high / len(shards))
        return jnp.repeat(jnp.exp(steps), dims[dim] // shards_of).reshape((-1,) + (1,) * (len(dims) - dim - 1))

    gain = one(*shards[0])
    for cut in shards[1:]:
        gain = gain * one(*cut)
    return gain


def scatter_about(own_key, shape, deviation, reach, split=(), held_as=jnp.bfloat16):
    factor_of = shard_levels(own_key, shape, split, -0.22, 0.18) if split else 1.0
    array = jax.random.normal(own_key, shape, jnp.float32) * deviation * factor_of
    return jnp.minimum(jnp.maximum(array, -reach), reach).astype(held_as)


def setup_inputs(seed: int = 0) -> dict:
    splits = jax.random.split(jax.random.key(seed), 6)
    b_aux = scatter_about(splits[0], (NAUX, NOCC, KW), 0.011, 0.06982422, ((0, 128),))
    eps_occ = jnp.clip(jax.random.uniform(splits[1], (NOCC,), jnp.float32, -3.0, -0.3), -3.0, -0.3)
    eps_vir = jnp.clip(jax.random.uniform(splits[2], (NVIR,), jnp.float32, 0.5, 3.0), 0.5, 3.0)
    domains = plant(jax.random.randint(splits[3], (NOCC, KMAX), 0, NVIR // VBLK), jax.random.fold_in(splits[3], 1), 0, (NVIR // VBLK) - 1).astype(jnp.int32)
    pair_keep = plant((jax.random.randint(splits[4], (NOCC, 2 * H + 1), 0, 4) < 3).astype(jnp.int32), jax.random.fold_in(splits[4], 1), 0, 1)
    return {"b_aux": b_aux, "eps_occ": eps_occ, "eps_vir": eps_vir, "domains": domains, "pair_keep": pair_keep}


def domain_energies(eps_vir, domains):
    offsets = jnp.arange(VBLK, dtype=jnp.int32)
    index = (domains[:, :, None] * VBLK + offsets[None, None, :]).reshape(domains.shape[0], KMAX * VBLK)
    return eps_vir[index]


def reference(b_aux, eps_occ, eps_vir, domains, pair_keep):
    nbatch = N_OCC
    per = OCC_DEV
    width = KMAX * VBLK
    whole = b_aux.astype(jnp.float32).reshape(NAUX, nbatch, per, width)
    energy_vir = domain_energies(eps_vir, domains).reshape(nbatch, per, width)
    energy_occ = eps_occ.reshape(nbatch, per)
    keep = pair_keep.astype(jnp.float32).reshape(nbatch, per, 2 * H + 1)
    gamma = jnp.zeros((NAUX, nbatch, per, width), jnp.float32)
    for offset in range(-H, H + 1):
        partner = jnp.roll(whole, offset, axis=1)
        vir_part = jnp.roll(energy_vir, offset, axis=0)
        occ_part = jnp.roll(energy_occ, offset, axis=0)
        coulomb = jnp.einsum('pbia,pbjc->biajc', whole, partner)
        denom = (energy_vir[:, :, :, None, None] + vir_part[:, None, None, :, :]
                 - energy_occ[:, :, None, None, None] - occ_part[:, None, None, :, None])
        rounded = lax.optimization_barrier((-coulomb / denom).astype(jnp.bfloat16))
        weight = keep[:, :, offset + H][:, :, None, None, None]
        amp = rounded.astype(jnp.float32) * weight
        gamma = gamma + jnp.einsum('biajc,pbjc->pbia', amp, partner)
    return gamma.astype(jnp.bfloat16).reshape(NAUX, nbatch * per, width)
```

```python
import jax
import jax.numpy as jnp
from jax import lax
from jax.experimental import pallas as pl
from jax.experimental.pallas import tpu as pltpu
from jax.sharding import PartitionSpec as P

MESH = pl.DeviceIdType.MESH
F32 = jnp.float32
BF16 = jnp.bfloat16

PB = 64
W = 512
NB = 32
OWN = 4
HALO = 3
LOC = OWN + HALO
NCODE = 8
PS = NCODE * PB
WIN = OWN * W
COLS = ((0, 640), (640, 640), (1280, 768))
RS_DTYPES = (BF16, F32, F32)


def side(pos):
    return lax.rem(lax.div(pos + 1, 2), 2)


def kernel(b_ref, evir_ref, eocc_ref, dom_ref, keep_ref, out_ref,
           b3, bg, bt, acc, s0, r0, s1, r1, s2, r2, s3, r3, mb, mm, gam, go, rr, kb, erow, ecol,
           loc_sem, a_send, a_recv, c_send, c_recv, rs_send, rs_recv, ag_send, ag_recv,
           gc_send, gc_recv, o_send, o_recv, k_send, k_recv):
    occ = lax.axis_index("occ")
    aux = lax.axis_index("aux")
    core = lax.rem(aux, 2)
    pos = (lax.div(occ, 8), lax.div(aux, 2) * 2 + lax.rem(lax.div(occ, 4), 2), lax.rem(occ, 4))
    half = tuple(lax.div(p, 2) for p in pos)
    fs = tuple(side(p) for p in pos)
    code = fs[0] * 4 + fs[1] * 2 + fs[2]

    def device(x, y, z, c):
        return (x * 8 + lax.rem(y, 2) * 4 + z, lax.div(y, 2) * 2 + c)

    group_peers = []
    for r in range(1, 8):
        bits = ((r >> 2) & 1, (r >> 1) & 1, r & 1)
        where = [p + 1 - 2 * lax.rem(p, 2) if bit else p for p, bit in zip(pos, bits)]
        flips = [1 - f if bit else f for f, bit in zip(fs, bits)]
        group_peers.append((device(*where, core), flips[0] * 4 + flips[1] * 2 + flips[2]))
    slice_peers = []
    for d in range(3):
        where = list(pos)
        where[d] = 3 - pos[d]
        slice_peers.append(device(*where, core))
    sibling = device(*pos, 1 - core)

    def remote(src, dst, send, recv, dev):
        return pltpu.make_async_remote_copy(
            src_ref=src, dst_ref=dst, send_sem=send, recv_sem=recv, device_id=dev, device_id_type=MESH)

    loads = [pltpu.make_async_copy(b_ref.at[:, o], b3.at[:, :, pl.ds(o * 256, 256)], loc_sem.at[o]) for o in range(2)]
    for cp in loads:
        cp.start()
    kslot = kb.at[half[2], half[0], code]
    kcopy = pltpu.make_async_copy(keep_ref, kslot, loc_sem.at[2])
    kcopy.start()

    barrier = pltpu.get_barrier_semaphore()
    everyone = [dev for dev, _ in group_peers] + slice_peers + [sibling]
    for dev in everyone:
        pl.semaphore_signal(barrier, inc=1, device_id=dev, device_id_type=MESH)
    for cp in loads:
        cp.wait()
    kcopy.wait()
    pl.semaphore_wait(barrier, len(everyone))

    first = code * OWN - HALO + NB

    def send_in(t, _):
        for dev, q in group_peers:
            batch = lax.rem(q * OWN - HALO + NB + t, NB)
            remote(b3.at[batch], bg.at[t, pl.ds(pl.multiple_of(code * PB, PB), PB)], a_send.at[0], a_recv.at[t], dev).start()
        return 0

    lax.fori_loop(0, LOC, send_in, 0)
    for dev, q in group_peers:
        remote(kslot, kslot, k_send.at[0], k_recv.at[0], dev).start()

    def own_rows(t, _):
        batch = lax.rem(first + t, NB)
        bg[t, pl.ds(pl.multiple_of(code * PB, PB), PB), :] = b3[batch]
        return 0

    lax.fori_loop(0, LOC, own_rows, 0)

    for t in range(LOC):
        for o in range(2):
            orb = lax.rem(first + t, NB) * 2 + o
            for k in range(2):
                row = evir_ref[dom_ref[orb, k]] - eocc_ref[orb]
                lane = t * W + o * 256 + k * 128
                erow[:, lane:lane + 128] = row
                if t >= HALO:
                    at = lane - HALO * W
                    ecol[at:at + 128, :] = jnp.broadcast_to(row, (128, 128)).T

    def keep_group():
        pltpu.make_async_copy(kb.at[0, 0, pl.ds(0, 7)], kb.at[0, 0, pl.ds(0, 7)], k_recv.at[0]).wait()
        pltpu.make_async_copy(kb.at[0, 0, pl.ds(0, 7)], kb.at[0, 0, pl.ds(0, 7)], k_send.at[0]).wait()

    def keep_x():
        ref = kb.at[half[2], half[0]]
        return remote(ref, ref, k_send.at[1], k_recv.at[1], slice_peers[0])

    def keep_z():
        ref = kb.at[half[2]]
        return remote(ref, ref, k_send.at[2], k_recv.at[2], slice_peers[2])

    def orders(u):
        return [(u + n) % 3 for n in range(3)]

    def band(ref, c, rows, size, u):
        lo, width = COLS[u]
        return ref.at[c, pl.ds(rows, size), pl.ds(lo, width)]

    def wait_in(t):
        pltpu.make_async_copy(bg.at[0, pl.ds(0, 7 * PB)], bg.at[0, pl.ds(0, 7 * PB)], a_recv.at[t]).wait()

    def core_copy(c):
        return remote(s0.at[c % 2], r0.at[c], c_send.at[c], c_recv.at[c], sibling)

    rs_bufs = ((s1, r1), (s2, r2), (s3, r3))

    def rs_copy(n, c, u):
        size = 128 >> n
        sb, rb = rs_bufs[n]
        return remote(band(sb, c % 2, 0, size, u), band(rb, c, 0, size, u),
                      rs_send.at[n, c, u], rs_recv.at[n, c, u], slice_peers[orders(u)[n]])

    def base_rows(u, n):
        at = core * 0
        for m in range(n):
            at = at + half[orders(u)[m]] * (128 >> m)
        return at

    def ag_copy(n, c, u):
        size = 128 >> n
        rows = pl.multiple_of(core * 256 + base_rows(u, n + 1), 32)
        ref = band(mb, c, rows, size, u)
        return remote(ref, ref, ag_send.at[n, c, u], ag_recv.at[n, c, u], slice_peers[orders(u)[n]])

    def gc_copy(c):
        ref = mb.at[c, pl.ds(pl.multiple_of(core * 256, 256), 256)]
        return remote(ref, ref, gc_send.at[c], gc_recv.at[c], sibling)

    def stage_v(c):
        top = HALO + c
        if c == 0:
            for t in range(HALO):
                wait_in(t)
        wait_in(top)
        if c >= 2:
            core_copy(c - 2).wait_send()
        for h in range(2):
            lanes = core * 256 if h == 0 else (1 - core) * 256
            bt[h] = bg[top, :, pl.ds(pl.multiple_of(lanes, 256), 256)].T

        def offset(s, _):
            at = pl.ds(pl.multiple_of(s * W, W), W)
            other = bg[top - s]
            s0[c % 2, :, at] = jnp.dot(bt[1], other, preferred_element_type=F32)
            acc[c, :, at] = jnp.dot(bt[0], other, preferred_element_type=F32)
            return 0

        lax.fori_loop(0, OWN, offset, 0)
        core_copy(c).start()

    def fold(src, send_to, n, c, u):
        size = 128 >> n
        lo, width = COLS[u]
        cols = slice(lo, lo + width)
        d = orders(u)[n]
        base = base_rows(u, n)
        keep_at = half[d] * size
        send_at = (1 - half[d]) * size
        step = 32

        def body(k, _):
            near = pl.ds(pl.multiple_of(send_at + k * step, step), step)
            mine = pl.ds(pl.multiple_of(base + send_at + k * step, step), step)
            val = acc[c, mine, cols] + src[c, near, cols].astype(F32)
            send_to[c % 2, pl.ds(pl.multiple_of(k * step, step), step), cols] = val.astype(send_to.dtype)
            return 0

        lax.fori_loop(0, size // step, body, 0)
        rs_copy(n, c, u).start()

        def body2(k, _):
            near = pl.ds(pl.multiple_of(keep_at + k * step, step), step)
            mine = pl.ds(pl.multiple_of(base + keep_at + k * step, step), step)
            acc[c, mine, cols] = acc[c, mine, cols] + src[c, near, cols].astype(F32)
            return 0

        lax.fori_loop(0, size // step, body2, 0)

    def stage_rs(n, c):
        if n == 0:
            core_copy(c).wait_recv()
        for u in range(3):
            if n > 0:
                rs_copy(n - 1, c, u).wait_recv()
            if c >= 2:
                rs_copy(n, c - 2, u).wait_send()
            fold(r0 if n == 0 else rs_bufs[n - 1][1], rs_bufs[n][0], n, c, u)

    def stage_amp(c):
        for u in range(3):
            rs_copy(2, c, u).wait_recv()
            lo, width = COLS[u]
            base = pl.multiple_of(base_rows(u, 3), 32)
            rows = ecol[pl.ds(pl.multiple_of(c * W + core * 256 + base, 32), 32), :]
            for k in range(width // 128):
                at = lo + k * 128
                s, lane = at // W, at % W
                total = acc[c, pl.ds(base, 32), at:at + 128] + r3[c, 0:32, at:at + 128]
                src = (HALO + c - s) * W + lane
                denom = rows + erow[:, src:src + 128]
                mb[c, pl.ds(pl.multiple_of(core * 256 + base, 32), 32), at:at + 128] = (-total / denom).astype(BF16)
            ag_copy(2, c, u).start()

    def stage_ag(n, c):
        for u in range(3):
            ag_copy(n + 1, c, u).wait_recv()
            ag_copy(n, c, u).start()

    def stage_gc(c):
        for u in range(3):
            ag_copy(0, c, u).wait_recv()
        gc_copy(c).start()

    def flag(batch, orbital, offset):
        y = half[1] * 2 + lax.rem(lax.div(batch, 4), 2)
        x, z = lax.div(batch, 8), lax.rem(batch, 4)
        q = side(x) * 4 + side(y) * 2 + side(z)
        row = orbital * LOC + offset
        line = kb[lax.div(z, 2), lax.div(x, 2), q, row:row + 1, :]
        return jnp.broadcast_to(line, (256, 128)).astype(BF16)

    def finish(t):
        go[t] = gam[t].astype(BF16)
        rr[code, t] = go[t, pl.ds(pl.multiple_of(code * PB, PB), PB)]
        for dev, q in group_peers:
            remote(go.at[t, pl.ds(pl.multiple_of(q * PB, PB), PB)], rr.at[code, t], o_send.at[0], o_recv.at[t], dev).start()

    def nt(a, b):
        return lax.dot_general(a, b, (((1,), (1,)), ((), ())), preferred_element_type=F32)

    def stage_gamma(c):
        top = HALO + c
        gc_copy(c).wait_recv()
        batch = lax.rem(first + top, NB)
        for s in range(1, OWN):
            other = lax.rem(first + top - s, NB)
            for o in range(2):
                m = flag(other, o, HALO - s)
                for k in range(2):
                    lanes = slice(s * W + o * 256 + k * 128, s * W + o * 256 + k * 128 + 128)
                    for h in range(2):
                        mm[h * 256:h * 256 + 256, lanes] = mb[c, h * 256:h * 256 + 256, lanes] * m
        for s in range(OWN - 1, 0, -1):
            t = top - s
            part = jnp.dot(bg[top], mm[:, s * W:s * W + W], preferred_element_type=F32)
            if c == 0 and t < HALO:
                gam[t] = part
            else:
                gam[t] = gam[t] + part
            if s == OWN - 1:
                finish(t)
            elif c == OWN - 1:
                finish(t)
        for s in range(OWN):
            for h in range(2):
                m = flag(batch, h, HALO + s)
                for k in range(4):
                    lanes = slice(s * W + k * 128, s * W + k * 128 + 128)
                    mm[h * 256:h * 256 + 256, lanes] = mb[c, h * 256:h * 256 + 256, lanes] * m
        part = nt(bg[top], mm[:, 0:W])
        for s in range(1, OWN):
            part = part + nt(bg[top - s], mm[:, s * W:s * W + W])
        gam[top] = part
        if c == OWN - 1:
            finish(top)

    stages = [
        stage_v,
        lambda c: stage_rs(0, c),
        lambda c: stage_rs(1, c),
        lambda c: stage_rs(2, c),
        stage_amp,
        lambda c: stage_ag(1, c),
        lambda c: stage_ag(0, c),
        stage_gc,
        stage_gamma,
    ]
    for tick in range(len(stages) + OWN - 1):
        for c in range(OWN):
            n = tick - c
            if 0 <= n < len(stages):
                stages[n](c)
        if tick == 0:
            keep_group()
            keep_x().start()
        if tick == 2:
            keep_x().wait()
            keep_z().start()
        if tick == 4:
            keep_z().wait()

    pltpu.make_async_copy(rr.at[pl.ds(0, 7)], rr.at[pl.ds(0, 7)], a_send.at[0]).wait()
    for c in range(OWN):
        if c >= 2:
            core_copy(c).wait_send()
        gc_copy(c).wait_send()
        for u in range(3):
            for n in range(3):
                if c >= 2:
                    rs_copy(n, c, u).wait_send()
                ag_copy(n, c, u).wait_send()

    for t in range(LOC):
        pltpu.make_async_copy(bg.at[0, pl.ds(0, 7 * PB)], bg.at[0, pl.ds(0, 7 * PB)], o_recv.at[t]).wait()

    def combine(g, _):
        nxt = lax.rem(g + 1, NCODE)
        b3[g * OWN] = rr[g, HALO]
        for k in range(1, OWN):
            b3[g * OWN + k] = (rr[g, HALO + k].astype(F32) + rr[nxt, k - 1].astype(F32)).astype(BF16)
        return 0

    lax.fori_loop(0, NCODE, combine, 0)
    stores = [pltpu.make_async_copy(b3.at[:, :, pl.ds(o * 256, 256)], out_ref.at[:, o], loc_sem.at[o]) for o in range(2)]
    for cp in stores:
        cp.start()
    for cp in stores:
        cp.wait()
    pltpu.make_async_copy(rr.at[pl.ds(0, 7)], rr.at[pl.ds(0, 7)], o_send.at[0]).wait()


def shards(b_aux, eps_occ, eps_vir, domains, pair_keep):
    rows = jnp.transpose(b_aux, (1, 0, 2)).reshape(NB, 2, PB, 256)
    keep = jnp.broadcast_to(pair_keep.astype(F32).reshape(2 * LOC, 1), (2 * LOC, 128))
    keep = jnp.pad(keep, ((0, 2), (0, 0)))
    dma, vm = pltpu.SemaphoreType.DMA, pltpu.VMEM
    hbm = pl.BlockSpec(memory_space=pl.ANY)
    vmem = pl.BlockSpec(memory_space=pltpu.VMEM)
    smem = pl.BlockSpec(memory_space=pltpu.SMEM)
    rs1, rs2, rs3 = RS_DTYPES
    out = pl.pallas_call(
        kernel,
        out_shape=jax.ShapeDtypeStruct((NB, 2, PB, 256), BF16),
        in_specs=[hbm, vmem, smem, smem, hbm],
        out_specs=hbm,
        scratch_shapes=[
            vm((NB, PB, W), BF16),
            vm((LOC, PS, W), BF16),
            vm((2, 256, PS), BF16),
            vm((OWN, 256, WIN), F32),
            vm((2, 256, WIN), F32), vm((OWN, 256, WIN), F32),
            vm((2, 128, WIN), rs1), vm((OWN, 128, WIN), rs1),
            vm((2, 64, WIN), rs2), vm((OWN, 64, WIN), rs2),
            vm((2, 32, WIN), rs3), vm((OWN, 32, WIN), rs3),
            vm((OWN, W, WIN), BF16),
            vm((W, WIN), BF16),
            vm((LOC, PS, W), F32),
            vm((LOC, PS, W), BF16),
            vm((NCODE, LOC, PB, W), BF16),
            vm((2, 2, NCODE, 16, 128), F32),
            vm((1, LOC * W), F32),
            vm((OWN * W, 128), F32),
            dma((3,)), dma((1,)), dma((LOC,)),
            dma((OWN,)), dma((OWN,)),
            dma((3, OWN, 3)), dma((3, OWN, 3)),
            dma((3, OWN, 3)), dma((3, OWN, 3)),
            dma((OWN,)), dma((OWN,)),
            dma((1,)), dma((LOC,)),
            dma((3,)), dma((3,)),
        ],
        compiler_params=pltpu.CompilerParams(
            collective_id=0, has_side_effects=True, vmem_limit_bytes=62 * 1024 * 1024),
    )(rows, eps_vir.reshape(32, 1, 128), eps_occ, domains, keep)
    return jnp.transpose(out.reshape(2 * NB, PB, 256), (1, 0, 2))


def solution(mesh):
    in_specs = (P(("occ", "aux"), None, None), P(), P(), P(), P("occ", None))
    out_specs = P(("occ", "aux"), None, None)
    return jax.shard_map(shards, mesh=mesh, in_specs=in_specs, out_specs=out_specs, check_vma=False)
```

```python
import functools

import jax
import jax.numpy as jnp
from jax import lax
from jax.experimental import pallas as pl
from jax.experimental.pallas import tpu as pltpu
from jax.sharding import PartitionSpec as P

MESH = pl.DeviceIdType.MESH
F32 = jnp.float32
BF16 = jnp.bfloat16

PB = 64
W = 512
NB = 32
OWN = 4
HALO = 3
LOC = OWN + HALO
NCODE = 8
PS = NCODE * PB
SLOTS = 4
ARRIVALS = (3, 4, 1, 0, 2, 5, 6)
UNITS = (
    (3, 1), (4, 2), (3, 3), (5, 1), (6, 2), (3, 0), (4, 1), (5, 2),
    (3, 2), (6, 3), (4, 0), (5, 3), (4, 3), (6, 0), (5, 0), (6, 1),
)
STEPS = (
    (0, 5), (1, 5), (0, 6), (0, 10), (1, 6), (2, 5), (1, 10), (0, 8), (0, 12), (1, 8), (2, 6), (1, 12),
    (2, 10), (3, 5), (0, 2), (3, 6), (1, 2), (4, 5), (2, 8), (2, 12), (3, 10), (4, 6), (0, 0), (5, 5),
    (0, 1), (3, 8), (3, 12), (1, 0), (2, 2), (4, 10), (1, 1), (5, 6), (6, 5), (4, 8), (0, 3), (4, 12),
    (0, 7), (0, 11), (0, 14), (2, 0), (1, 3), (1, 7), (2, 1), (3, 2), (1, 11), (5, 10), (6, 6), (1, 14),
    (7, 5), (5, 8), (5, 12), (0, 4), (8, 5), (3, 0), (3, 1), (1, 4), (2, 3), (2, 7), (2, 11), (4, 2),
    (7, 6), (0, 9), (6, 10), (6, 12), (8, 6), (6, 8), (1, 9), (4, 1), (2, 14), (2, 4), (3, 11), (4, 0),
    (3, 3), (5, 2), (3, 7), (7, 12), (0, 13), (8, 12), (7, 10), (0, 15), (7, 8), (1, 13), (2, 9), (8, 10),
    (5, 1), (3, 4), (4, 11), (1, 15), (5, 0), (8, 8), (4, 3), (3, 14), (6, 2), (4, 7), (6, 1), (2, 13),
    (4, 4), (5, 3), (3, 9), (5, 11), (6, 0), (2, 15), (7, 2), (5, 7), (4, 14), (5, 4), (8, 2), (6, 11),
    (3, 13), (4, 9), (7, 1), (6, 7), (8, 1), (7, 0), (6, 3), (6, 4), (3, 15), (4, 13), (8, 0), (5, 14),
    (7, 11), (5, 9), (8, 11), (7, 7), (4, 15), (7, 3), (5, 13), (8, 7), (7, 4), (8, 3), (6, 14), (6, 9),
    (8, 4), (5, 15), (6, 13), (7, 14), (7, 9), (6, 15), (8, 14), (8, 9), (7, 13), (8, 13), (7, 15), (8, 15),
)
RS_DTYPES = (BF16, BF16, F32)


def side(pos):
    return lax.rem(lax.div(pos + 1, 2), 2)


def kernel(steps, arrivals, units, b_ref, evir_ref, eocc_ref, dom_ref, keep_ref, out_ref,
           b3, bg, bt, acc, s0, r0, s1, r1, s2, r2, s3, r3, mb, mm, gam, go, rr, kb, erow, ecol,
           loc_sem, out_sem, a_send, a_recv, c_send, c_recv, rs_send, rs_recv, ag_send, ag_recv,
           gc_send, gc_recv, o_send, o_recv, k_send, k_recv):
    occ = lax.axis_index("occ")
    aux = lax.axis_index("aux")
    core = lax.rem(aux, 2)
    pos = (lax.div(occ, 8), lax.div(aux, 2) * 2 + lax.rem(lax.div(occ, 4), 2), lax.rem(occ, 4))
    half = tuple(lax.div(p, 2) for p in pos)
    fs = tuple(side(p) for p in pos)
    code = fs[0] * 4 + fs[1] * 2 + fs[2]

    def device(x, y, z, c):
        return (x * 8 + lax.rem(y, 2) * 4 + z, lax.div(y, 2) * 2 + c)

    group_peers = []
    for r in range(1, 8):
        bits = ((r >> 2) & 1, (r >> 1) & 1, r & 1)
        where = [p + 1 - 2 * lax.rem(p, 2) if bit else p for p, bit in zip(pos, bits)]
        flips = [1 - f if bit else f for f, bit in zip(fs, bits)]
        group_peers.append((device(*where, core), flips[0] * 4 + flips[1] * 2 + flips[2]))
    slice_peers = []
    for d in range(3):
        where = list(pos)
        where[d] = 3 - pos[d]
        slice_peers.append(device(*where, core))
    sibling = device(*pos, 1 - core)

    def remote(src, dst, send, recv, dev):
        return pltpu.make_async_remote_copy(
            src_ref=src, dst_ref=dst, send_sem=send, recv_sem=recv, device_id=dev, device_id_type=MESH)

    loads = [pltpu.make_async_copy(b_ref.at[:, o], b3.at[:, :, pl.ds(o * 256, 256)], loc_sem.at[o]) for o in range(2)]
    for cp in loads:
        cp.start()
    kslot = kb.at[half[2], half[0], code]
    for o in range(2):
        for k in range(LOC):
            kslot[o * LOC + k:o * LOC + k + 1, :] = jnp.full((1, 128), keep_ref[k, o].astype(F32))

    barrier = pltpu.get_barrier_semaphore()
    everyone = [dev for dev, _ in group_peers] + slice_peers + [sibling]
    for dev in everyone:
        pl.semaphore_signal(barrier, inc=1, device_id=dev, device_id_type=MESH)
    for cp in loads:
        cp.wait()
    pl.semaphore_wait(barrier, len(everyone))

    first = code * OWN - HALO + NB

    def send_in(t):
        for dev, q in group_peers:
            batch = lax.rem(q * OWN - HALO + NB + t, NB)
            remote(b3.at[batch], bg.at[t, pl.ds(pl.multiple_of(code * PB, PB), PB)], a_send.at[0], a_recv.at[t], dev).start()

    for t in arrivals:
        send_in(t)
    for dev, q in group_peers:
        remote(kslot, kslot, k_send.at[0], k_recv.at[0], dev).start()

    def own_rows(t, _):
        batch = lax.rem(first + t, NB)
        bg[t, pl.ds(pl.multiple_of(code * PB, PB), PB), :] = b3[batch]
        return 0

    lax.fori_loop(0, LOC, own_rows, 0)

    for t in range(LOC):
        for o in range(2):
            orb = lax.rem(first + t, NB) * 2 + o
            for k in range(2):
                row = evir_ref[dom_ref[k, orb]] - eocc_ref[orb]
                lane = t * W + o * 256 + k * 128
                erow[:, lane:lane + 128] = row
                if t >= HALO:
                    at = lane - HALO * W
                    ecol[at:at + 128, :] = jnp.broadcast_to(row, (128, 128)).T

    def keep_group():
        pltpu.make_async_copy(kb.at[0, 0, pl.ds(0, 7)], kb.at[0, 0, pl.ds(0, 7)], k_recv.at[0]).wait()
        pltpu.make_async_copy(kb.at[0, 0, pl.ds(0, 7)], kb.at[0, 0, pl.ds(0, 7)], k_send.at[0]).wait()

    def keep_x():
        ref = kb.at[half[2], half[0]]
        return remote(ref, ref, k_send.at[1], k_recv.at[1], slice_peers[0])

    def keep_z():
        ref = kb.at[half[2]]
        return remote(ref, ref, k_send.at[2], k_recv.at[2], slice_peers[2])

    def order(u, n):
        return (u + n) % 3

    def wait_in(t):
        pltpu.make_async_copy(bg.at[0, pl.ds(0, 7 * PB)], bg.at[0, pl.ds(0, 7 * PB)], a_recv.at[t]).wait()

    arrived, turned, touched = set(), set(), set()
    started = []
    left = [0] * LOC
    for top, s in units:
        left[top] += 1
        if s:
            left[top - s] += 1

    def core_copy(u):
        return remote(s0.at[started.index(u) % SLOTS], r0.at[u], c_send.at[u], c_recv.at[u], sibling)

    rs_bufs = ((s1, r1), (s2, r2), (s3, r3))

    def rs_copy(n, u):
        sb, rb = rs_bufs[n]
        return remote(sb.at[u], rb.at[u], rs_send.at[n, u], rs_recv.at[n, u], slice_peers[order(u, n)])

    def base_rows(u, n):
        at = core * 0
        for m in range(n):
            at = at + half[order(u, m)] * (128 >> m)
        return at

    def ag_copy(n, u):
        size = 128 >> n
        ref = mb.at[u, pl.ds(pl.multiple_of(core * 256 + base_rows(u, n + 1), 32), size)]
        return remote(ref, ref, ag_send.at[n, u], ag_recv.at[n, u], slice_peers[order(u, n)])

    def gc_copy(u):
        ref = mb.at[u, pl.ds(pl.multiple_of(core * 256, 256), 256)]
        return remote(ref, ref, gc_send.at[u], gc_recv.at[u], sibling)

    def stage_v(u):
        top, s = units[u]
        for t in (top, top - s):
            if t not in arrived:
                wait_in(t)
                arrived.add(t)
        own = top - HALO
        if top not in turned:
            turned.add(top)
            for h in range(2):
                lanes = core * 256 if h == 0 else (1 - core) * 256
                bt[own, h] = bg[top, :, pl.ds(pl.multiple_of(lanes, 256), 256)].T
        if len(started) >= SLOTS:
            core_copy(started[-SLOTS]).wait_send()
        started.append(u)
        other = bg[top - s]
        s0[started.index(u) % SLOTS] = jnp.dot(bt[own, 1], other, preferred_element_type=F32)
        core_copy(u).start()
        acc[u] = jnp.dot(bt[own, 0], other, preferred_element_type=F32)

    def fold(n, u):
        src = r0 if n == 0 else rs_bufs[n - 1][1]
        if n == 0:
            core_copy(u).wait_recv()
        else:
            rs_copy(n - 1, u).wait_recv()
        size = 128 >> n
        near_half = half[order(u, n)]
        base = base_rows(u, n)
        keep_at = near_half * size
        send_at = (1 - near_half) * size
        send_to = rs_bufs[n][0]
        step = 32

        def far(k, _):
            near = pl.ds(pl.multiple_of(send_at + k * step, step), step)
            mine = pl.ds(pl.multiple_of(base + send_at + k * step, step), step)
            val = acc[u, mine, :] + src[u, near, :].astype(F32)
            send_to[u, pl.ds(pl.multiple_of(k * step, step), step), :] = val.astype(send_to.dtype)
            return 0

        lax.fori_loop(0, size // step, far, 0)
        rs_copy(n, u).start()

        def stay(k, _):
            near = pl.ds(pl.multiple_of(keep_at + k * step, step), step)
            mine = pl.ds(pl.multiple_of(base + keep_at + k * step, step), step)
            acc[u, mine, :] = acc[u, mine, :] + src[u, near, :].astype(F32)
            return 0

        lax.fori_loop(0, size // step, stay, 0)

    def stage_amp(u):
        rs_copy(2, u).wait_recv()
        top, s = units[u]
        base = pl.multiple_of(base_rows(u, 3), 32)
        rows = ecol[pl.ds(pl.multiple_of((top - HALO) * W + core * 256 + base, 32), 32), :]
        for k in range(W // 128):
            lanes = slice(k * 128, k * 128 + 128)
            at = (top - s) * W + k * 128
            total = acc[u, pl.ds(base, 32), lanes] + r3[u, :, lanes]
            denom = rows + erow[:, at:at + 128]
            mb[u, pl.ds(pl.multiple_of(core * 256 + base, 32), 32), lanes] = (-total / denom).astype(BF16)
        ag_copy(2, u).start()

    def stage_ag(n, u):
        ag_copy(n + 1, u).wait_recv()
        ag_copy(n, u).start()

    def stage_gc(u):
        ag_copy(0, u).wait_recv()
        gc_copy(u).start()

    def flag(t, orbital, offset):
        batch = lax.rem(first + t, NB)
        y = half[1] * 2 + lax.rem(lax.div(batch, 4), 2)
        x, z = lax.div(batch, 8), lax.rem(batch, 4)
        q = side(x) * 4 + side(y) * 2 + side(z)
        row = orbital * LOC + offset
        line = kb[lax.div(z, 2), lax.div(x, 2), q, row:row + 1, :]
        return jnp.broadcast_to(line, (256, 128)).astype(BF16)

    finished = []

    def finish(t):
        finished.append(t)
        go[t] = gam[t].astype(BF16)
        for dev, q in group_peers:
            remote(go.at[t, pl.ds(pl.multiple_of(q * PB, PB), PB)], rr.at[code, t], o_send.at[0], o_recv.at[t], dev).start()
        rr[code, t] = go[t, pl.ds(pl.multiple_of(code * PB, PB), PB)]

    def add_term(t, part):
        if t in touched:
            gam[t] = gam[t] + part
        else:
            touched.add(t)
            gam[t] = part
        left[t] -= 1
        if left[t] == 0:
            finish(t)

    def stage_gamma(u):
        top, s = units[u]
        gc_copy(u).wait_recv()
        if s:
            for o in range(2):
                m = flag(top - s, o, HALO - s)
                for k in range(2):
                    lanes = slice(o * 256 + k * 128, o * 256 + k * 128 + 128)
                    for h in range(2):
                        mm[0, h * 256:h * 256 + 256, lanes] = mb[u, h * 256:h * 256 + 256, lanes] * m
            add_term(top - s, jnp.dot(bg[top], mm[0], preferred_element_type=F32))
        for h in range(2):
            m = flag(top, h, HALO + s)
            for k in range(4):
                lanes = slice(k * 128, k * 128 + 128)
                mm[1, h * 256:h * 256 + 256, lanes] = mb[u, h * 256:h * 256 + 256, lanes] * m
        add_term(top, lax.dot_general(bg[top - s], mm[1], (((1,), (1,)), ((), ())), preferred_element_type=F32))

    stages = [
        stage_v,
        lambda u: fold(0, u),
        lambda u: fold(1, u),
        lambda u: fold(2, u),
        stage_amp,
        lambda u: stage_ag(1, u),
        lambda u: stage_ag(0, u),
        stage_gc,
        stage_gamma,
    ]
    seen = set()
    for stage, u in steps:
        if stage not in seen:
            if stage == 1:
                keep_group()
                keep_x().start()
            if stage == 4:
                keep_x().wait()
                keep_z().start()
            if stage == 8:
                keep_z().wait()
        seen.add(stage)
        stages[stage](u)

    pltpu.make_async_copy(rr.at[pl.ds(0, 7)], rr.at[pl.ds(0, 7)], a_send.at[0]).wait()
    for at, u in enumerate(started):
        if at >= len(started) - SLOTS:
            core_copy(u).wait_send()
        gc_copy(u).wait_send()
        for n in range(3):
            rs_copy(n, u).wait_send()
            ag_copy(n, u).wait_send()

    got, done = set(), set()
    stores = []
    for t in finished:
        pltpu.make_async_copy(bg.at[0, pl.ds(0, 7 * PB)], bg.at[0, pl.ds(0, 7 * PB)], o_recv.at[t]).wait()
        got.add(t)
        for k in range(OWN):
            if k in done or HALO + k not in got or (k and k - 1 not in got):
                continue
            done.add(k)
            if k:
                def combine(g, _, k=k):
                    nxt = lax.rem(g + 1, NCODE)
                    rr[g, HALO + k] = (rr[g, HALO + k].astype(F32) + rr[nxt, k - 1].astype(F32)).astype(BF16)
                    return 0

                lax.fori_loop(0, NCODE, combine, 0)
            for o in range(2):
                cp = pltpu.make_async_copy(rr.at[:, HALO + k, :, pl.ds(o * 256, 256)], out_ref.at[:, k, o], out_sem.at[k, o])
                cp.start()
                stores.append(cp)
    for cp in stores:
        cp.wait()
    pltpu.make_async_copy(rr.at[pl.ds(0, 7)], rr.at[pl.ds(0, 7)], o_send.at[0]).wait()


def shards(b_aux, eps_occ, eps_vir, domains, pair_keep):
    rows = jnp.transpose(b_aux, (1, 0, 2)).reshape(NB, 2, PB, 256)
    dma, vm = pltpu.SemaphoreType.DMA, pltpu.VMEM
    hbm = pl.BlockSpec(memory_space=pl.ANY)
    vmem = pl.BlockSpec(memory_space=pltpu.VMEM)
    smem = pl.BlockSpec(memory_space=pltpu.SMEM)
    rs1, rs2, rs3 = RS_DTYPES
    n = len(UNITS)
    out = pl.pallas_call(
        functools.partial(kernel, STEPS, ARRIVALS, UNITS),
        out_shape=jax.ShapeDtypeStruct((NCODE, OWN, 2, PB, 256), BF16),
        in_specs=[hbm, vmem, smem, smem, smem],
        out_specs=hbm,
        scratch_shapes=[
            vm((NB, PB, W), BF16),
            vm((LOC, PS, W), BF16),
            vm((OWN, 2, 256, PS), BF16),
            vm((n, 256, W), F32),
            vm((SLOTS, 256, W), F32), vm((n, 256, W), F32),
            vm((n, 128, W), rs1), vm((n, 128, W), rs1),
            vm((n, 64, W), rs2), vm((n, 64, W), rs2),
            vm((n, 32, W), rs3), vm((n, 32, W), rs3),
            vm((n, W, W), BF16),
            vm((2, W, W), BF16),
            vm((LOC, PS, W), F32),
            vm((LOC, PS, W), BF16),
            vm((NCODE, LOC, PB, W), BF16),
            vm((2, 2, NCODE, 16, 128), F32),
            vm((1, LOC * W), F32),
            vm((OWN * W, 128), F32),
            dma((2,)), dma((OWN, 2)), dma((1,)), dma((LOC,)),
            dma((n,)), dma((n,)),
            dma((3, n)), dma((3, n)),
            dma((3, n)), dma((3, n)),
            dma((n,)), dma((n,)),
            dma((1,)), dma((LOC,)),
            dma((3,)), dma((3,)),
        ],
        compiler_params=pltpu.CompilerParams(
            collective_id=0, has_side_effects=True, vmem_limit_bytes=62 * 1024 * 1024),
    )(rows, eps_vir.reshape(32, 1, 128), eps_occ, domains.T, pair_keep.T)
    return jnp.transpose(out.reshape(2 * NB, PB, 256), (1, 0, 2))


def solution(mesh):
    in_specs = (P(("occ", "aux"), None, None), P(), P(), P(), P("occ", None))
    out_specs = P(("occ", "aux"), None, None)
    return jax.shard_map(shards, mesh=mesh, in_specs=in_specs, out_specs=out_specs, check_vma=False)
```

```python
import functools

import jax
import jax.numpy as jnp
from jax import lax
from jax.experimental import pallas as pl
from jax.experimental.pallas import tpu as pltpu
from jax.sharding import PartitionSpec as P

MESH = pl.DeviceIdType.MESH
F32 = jnp.float32
BF16 = jnp.bfloat16

PB = 64
W = 512
NB = 32
OWN = 4
HALO = 3
LOC = OWN + HALO
NCODE = 8
PS = NCODE * PB
SLOTS = 4
ARRIVALS = (4, 1, 3, 0, 2, 5, 6)
UNITS = (
    (3, 3), (3, 1), (4, 2), (6, 3), (5, 0), (4, 3), (5, 3), (5, 1),
    (5, 2), (3, 0), (6, 1), (4, 1), (4, 0), (3, 2), (6, 0), (6, 2),
)
STEPS = (
    (0, 12), (1, 12), (0, 5), (1, 5), (2, 12), (0, 9), (0, 11), (0, 13), (1, 9), (3, 12), (1, 11), (2, 5),
    (1, 13), (0, 0), (4, 12), (1, 0), (2, 9), (2, 11), (3, 5), (2, 13), (5, 12), (0, 1), (0, 2), (1, 1),
    (3, 9), (1, 2), (2, 0), (4, 5), (3, 13), (3, 11), (6, 12), (0, 4), (0, 6), (0, 7), (0, 8), (1, 4),
    (4, 9), (4, 13), (1, 6), (2, 1), (1, 7), (2, 2), (3, 0), (1, 8), (5, 5), (7, 12), (4, 11), (0, 3),
    (0, 10), (5, 9), (8, 12), (1, 3), (5, 13), (0, 14), (3, 1), (1, 10), (0, 15), (4, 0), (2, 4), (2, 6),
    (1, 14), (1, 15), (3, 2), (2, 7), (2, 8), (6, 13), (5, 11), (6, 5), (6, 9), (5, 0), (3, 4), (2, 3),
    (4, 1), (2, 10), (3, 6), (2, 14), (4, 2), (2, 15), (3, 7), (3, 8), (7, 13), (6, 11), (7, 5), (8, 13),
    (6, 0), (8, 5), (3, 3), (4, 6), (7, 9), (3, 10), (5, 2), (4, 4), (5, 1), (8, 9), (3, 15), (4, 8),
    (7, 11), (3, 14), (4, 7), (4, 3), (8, 11), (5, 6), (6, 1), (5, 8), (7, 0), (4, 15), (4, 14), (4, 10),
    (5, 3), (8, 0), (6, 2), (5, 4), (6, 6), (5, 7), (5, 15), (6, 8), (5, 10), (7, 1), (5, 14), (8, 1),
    (7, 2), (6, 3), (7, 6), (8, 2), (6, 4), (8, 6), (6, 7), (6, 14), (6, 15), (7, 8), (7, 3), (8, 8),
    (8, 3), (7, 4), (6, 10), (7, 15), (7, 14), (8, 4), (7, 7), (8, 14), (8, 15), (8, 7), (7, 10), (8, 10),
)
RS_DTYPES = (BF16, BF16, BF16)


def side(pos):
    return lax.rem(lax.div(pos + 1, 2), 2)


def kernel(steps, arrivals, units, b_ref, evir_ref, eocc_ref, dom_ref, keep_ref, out_ref,
           b3, bg, bt, acc, s0, r0, s1, r1, s2, r2, s3, r3, mb, mm, gam, go, rr, kb, erow, ecol,
           loc_sem, out_sem, a_send, a_recv, c_send, c_recv, rs_send, rs_recv, ag_send, ag_recv,
           gc_send, gc_recv, o_send, o_recv, k_send, k_recv):
    occ = lax.axis_index("occ")
    aux = lax.axis_index("aux")
    core = lax.rem(aux, 2)
    pos = (lax.div(occ, 8), lax.div(aux, 2) * 2 + lax.rem(lax.div(occ, 4), 2), lax.rem(occ, 4))
    half = tuple(lax.div(p, 2) for p in pos)
    fs = tuple(side(p) for p in pos)
    code = fs[0] * 4 + fs[1] * 2 + fs[2]

    def device(x, y, z, c):
        return (x * 8 + lax.rem(y, 2) * 4 + z, lax.div(y, 2) * 2 + c)

    group_peers = []
    for r in range(1, 8):
        bits = ((r >> 2) & 1, (r >> 1) & 1, r & 1)
        where = [p + 1 - 2 * lax.rem(p, 2) if bit else p for p, bit in zip(pos, bits)]
        flips = [1 - f if bit else f for f, bit in zip(fs, bits)]
        group_peers.append((device(*where, core), flips[0] * 4 + flips[1] * 2 + flips[2]))
    slice_peers = []
    for d in range(3):
        where = list(pos)
        where[d] = 3 - pos[d]
        slice_peers.append(device(*where, core))
    sibling = device(*pos, 1 - core)

    def remote(src, dst, send, recv, dev):
        return pltpu.make_async_remote_copy(
            src_ref=src, dst_ref=dst, send_sem=send, recv_sem=recv, device_id=dev, device_id_type=MESH)

    loads = [pltpu.make_async_copy(b_ref.at[:, o], b3.at[:, :, pl.ds(o * 256, 256)], loc_sem.at[o]) for o in range(2)]
    for cp in loads:
        cp.start()
    kslot = kb.at[half[2], half[0], code]
    for o in range(2):
        for k in range(LOC):
            kslot[o * LOC + k:o * LOC + k + 1, :] = jnp.full((1, 128), keep_ref[o, k].astype(F32))

    barrier = pltpu.get_barrier_semaphore()
    everyone = [dev for dev, _ in group_peers] + slice_peers + [sibling]
    for dev in everyone:
        pl.semaphore_signal(barrier, inc=1, device_id=dev, device_id_type=MESH)
    for cp in loads:
        cp.wait()
    pl.semaphore_wait(barrier, len(everyone))

    first = code * OWN - HALO + NB

    def send_in(t):
        for dev, q in group_peers:
            batch = lax.rem(q * OWN - HALO + NB + t, NB)
            remote(b3.at[batch], bg.at[t, pl.ds(pl.multiple_of(code * PB, PB), PB)], a_send.at[0], a_recv.at[t], dev).start()

    for dev, q in group_peers:
        remote(kslot, kslot, k_send.at[0], k_recv.at[0], dev).start()
    for t in arrivals:
        send_in(t)

    def own_rows(t, _):
        batch = lax.rem(first + t, NB)
        bg[t, pl.ds(pl.multiple_of(code * PB, PB), PB), :] = b3[batch]
        return 0

    lax.fori_loop(0, LOC, own_rows, 0)

    for t in range(LOC):
        for o in range(2):
            orb = lax.rem(first + t, NB) * 2 + o
            for k in range(2):
                row = evir_ref[dom_ref[k, orb]] - eocc_ref[orb]
                lane = t * W + o * 256 + k * 128
                erow[:, lane:lane + 128] = row
                if t >= HALO:
                    at = lane - HALO * W
                    ecol[at:at + 128, :] = jnp.broadcast_to(row, (128, 128)).T

    def keep_group():
        pltpu.make_async_copy(kb.at[0, 0, pl.ds(0, 7)], kb.at[0, 0, pl.ds(0, 7)], k_recv.at[0]).wait()
        pltpu.make_async_copy(kb.at[0, 0, pl.ds(0, 7)], kb.at[0, 0, pl.ds(0, 7)], k_send.at[0]).wait()

    def keep_x():
        ref = kb.at[half[2], half[0]]
        return remote(ref, ref, k_send.at[1], k_recv.at[1], slice_peers[0])

    def keep_z():
        ref = kb.at[half[2]]
        return remote(ref, ref, k_send.at[2], k_recv.at[2], slice_peers[2])

    def order(u, n):
        return (u + n) % 3

    def wait_in(t):
        pltpu.make_async_copy(bg.at[0, pl.ds(0, 7 * PB)], bg.at[0, pl.ds(0, 7 * PB)], a_recv.at[t]).wait()

    arrived, turned, touched = set(), set(), set()
    started = []
    left = [0] * LOC
    for top, s in units:
        left[top] += 1
        if s:
            left[top - s] += 1

    def core_copy(u):
        return remote(s0.at[started.index(u) % SLOTS], r0.at[u], c_send.at[u], c_recv.at[u], sibling)

    rs_bufs = ((s1, r1), (s2, r2), (s3, r3))

    def rs_copy(n, u):
        sb, rb = rs_bufs[n]
        return remote(sb.at[u], rb.at[u], rs_send.at[n, u], rs_recv.at[n, u], slice_peers[order(u, n)])

    def base_rows(u, n):
        at = core * 0
        for m in range(n):
            at = at + half[order(u, m)] * (128 >> m)
        return at

    def ag_copy(n, u):
        size = 128 >> n
        ref = mb.at[u, pl.ds(pl.multiple_of(core * 256 + base_rows(u, n + 1), 32), size)]
        return remote(ref, ref, ag_send.at[n, u], ag_recv.at[n, u], slice_peers[order(u, n)])

    def gc_copy(u):
        ref = mb.at[u, pl.ds(pl.multiple_of(core * 256, 256), 256)]
        return remote(ref, ref, gc_send.at[u], gc_recv.at[u], sibling)

    def stage_v(u):
        top, s = units[u]
        for t in (top, top - s):
            if t not in arrived:
                wait_in(t)
                arrived.add(t)
        own = top - HALO
        if top not in turned:
            turned.add(top)
            for h in range(2):
                lanes = core * 256 if h == 0 else (1 - core) * 256
                bt[own, h] = bg[top, :, pl.ds(pl.multiple_of(lanes, 256), 256)].T
        if len(started) >= SLOTS:
            core_copy(started[-SLOTS]).wait_send()
        started.append(u)
        other = bg[top - s]
        s0[started.index(u) % SLOTS] = jnp.dot(bt[own, 1], other, preferred_element_type=F32)
        core_copy(u).start()
        acc[u] = jnp.dot(bt[own, 0], other, preferred_element_type=F32)

    def fold(n, u):
        src = r0 if n == 0 else rs_bufs[n - 1][1]
        if n == 0:
            core_copy(u).wait_recv()
        else:
            rs_copy(n - 1, u).wait_recv()
        size = 128 >> n
        near_half = half[order(u, n)]
        base = base_rows(u, n)
        keep_at = near_half * size
        send_at = (1 - near_half) * size
        send_to = rs_bufs[n][0]
        step = 32

        def far(k, _):
            near = pl.ds(pl.multiple_of(send_at + k * step, step), step)
            mine = pl.ds(pl.multiple_of(base + send_at + k * step, step), step)
            val = acc[u, mine, :] + src[u, near, :].astype(F32)
            send_to[u, pl.ds(pl.multiple_of(k * step, step), step), :] = val.astype(send_to.dtype)
            return 0

        lax.fori_loop(0, size // step, far, 0)
        rs_copy(n, u).start()

        def stay(k, _):
            near = pl.ds(pl.multiple_of(keep_at + k * step, step), step)
            mine = pl.ds(pl.multiple_of(base + keep_at + k * step, step), step)
            acc[u, mine, :] = acc[u, mine, :] + src[u, near, :].astype(F32)
            return 0

        lax.fori_loop(0, size // step, stay, 0)

    def stage_amp(u):
        rs_copy(2, u).wait_recv()
        top, s = units[u]
        base = pl.multiple_of(base_rows(u, 3), 32)
        rows = ecol[pl.ds(pl.multiple_of((top - HALO) * W + core * 256 + base, 32), 32), :]
        for k in range(W // 128):
            lanes = slice(k * 128, k * 128 + 128)
            at = (top - s) * W + k * 128
            total = acc[u, pl.ds(base, 32), lanes] + r3[u, :, lanes]
            denom = rows + erow[:, at:at + 128]
            mb[u, pl.ds(pl.multiple_of(core * 256 + base, 32), 32), lanes] = (-total / denom).astype(BF16)
        ag_copy(2, u).start()

    def stage_ag(n, u):
        ag_copy(n + 1, u).wait_recv()
        ag_copy(n, u).start()

    def stage_gc(u):
        ag_copy(0, u).wait_recv()
        gc_copy(u).start()

    def flag(t, orbital, offset):
        batch = lax.rem(first + t, NB)
        y = half[1] * 2 + lax.rem(lax.div(batch, 4), 2)
        x, z = lax.div(batch, 8), lax.rem(batch, 4)
        q = side(x) * 4 + side(y) * 2 + side(z)
        row = orbital * LOC + offset
        line = kb[lax.div(z, 2), lax.div(x, 2), q, row:row + 1, :]
        return jnp.broadcast_to(line, (256, 128)).astype(BF16)

    finished = []

    def finish(t):
        finished.append(t)
        go[t] = gam[t].astype(BF16)
        for dev, q in group_peers:
            remote(go.at[t, pl.ds(pl.multiple_of(q * PB, PB), PB)], rr.at[code, t], o_send.at[0], o_recv.at[t], dev).start()
        rr[code, t] = go[t, pl.ds(pl.multiple_of(code * PB, PB), PB)]

    def add_term(t, part):
        if t in touched:
            gam[t] = gam[t] + part
        else:
            touched.add(t)
            gam[t] = part
        left[t] -= 1
        if left[t] == 0:
            finish(t)

    def stage_gamma(u):
        top, s = units[u]
        gc_copy(u).wait_recv()
        if s:
            for o in range(2):
                m = flag(top - s, o, HALO - s)
                for k in range(2):
                    lanes = slice(o * 256 + k * 128, o * 256 + k * 128 + 128)
                    for h in range(2):
                        mm[0, h * 256:h * 256 + 256, lanes] = mb[u, h * 256:h * 256 + 256, lanes] * m
            add_term(top - s, jnp.dot(bg[top], mm[0], preferred_element_type=F32))
        for h in range(2):
            m = flag(top, h, HALO + s)
            for k in range(4):
                lanes = slice(k * 128, k * 128 + 128)
                mm[1, h * 256:h * 256 + 256, lanes] = mb[u, h * 256:h * 256 + 256, lanes] * m
        add_term(top, lax.dot_general(bg[top - s], mm[1], (((1,), (1,)), ((), ())), preferred_element_type=F32))

    stages = [
        stage_v,
        lambda u: fold(0, u),
        lambda u: fold(1, u),
        lambda u: fold(2, u),
        stage_amp,
        lambda u: stage_ag(1, u),
        lambda u: stage_ag(0, u),
        stage_gc,
        stage_gamma,
    ]
    seen = set()
    for stage, u in steps:
        if stage not in seen:
            if stage == 1:
                keep_group()
                keep_x().start()
            if stage == 4:
                keep_x().wait()
                keep_z().start()
            if stage == 8:
                keep_z().wait()
        seen.add(stage)
        stages[stage](u)

    pltpu.make_async_copy(rr.at[pl.ds(0, 7)], rr.at[pl.ds(0, 7)], a_send.at[0]).wait()
    for at, u in enumerate(started):
        if at >= len(started) - SLOTS:
            core_copy(u).wait_send()
        gc_copy(u).wait_send()
        for n in range(3):
            rs_copy(n, u).wait_send()
            ag_copy(n, u).wait_send()

    got, done = set(), set()
    stores = []
    for t in finished:
        pltpu.make_async_copy(bg.at[0, pl.ds(0, 7 * PB)], bg.at[0, pl.ds(0, 7 * PB)], o_recv.at[t]).wait()
        got.add(t)
        for k in range(OWN):
            if k in done or HALO + k not in got or (k and k - 1 not in got):
                continue
            done.add(k)
            if k:
                def combine(g, _, k=k):
                    nxt = lax.rem(g + 1, NCODE)
                    rr[g, HALO + k] = (rr[g, HALO + k].astype(F32) + rr[nxt, k - 1].astype(F32)).astype(BF16)
                    return 0

                lax.fori_loop(0, NCODE, combine, 0)
            for o in range(2):
                cp = pltpu.make_async_copy(rr.at[:, HALO + k, :, pl.ds(o * 256, 256)], out_ref.at[:, k, o], out_sem.at[k, o])
                cp.start()
                stores.append(cp)
    for cp in stores:
        cp.wait()
    pltpu.make_async_copy(rr.at[pl.ds(0, 7)], rr.at[pl.ds(0, 7)], o_send.at[0]).wait()


def shards(b_aux, eps_occ, eps_vir, domains, pair_keep):
    rows = jnp.transpose(b_aux, (1, 0, 2)).reshape(NB, 2, PB, 256)
    dma, vm = pltpu.SemaphoreType.DMA, pltpu.VMEM
    hbm = pl.BlockSpec(memory_space=pl.ANY)
    vmem = pl.BlockSpec(memory_space=pltpu.VMEM)
    smem = pl.BlockSpec(memory_space=pltpu.SMEM)
    rs1, rs2, rs3 = RS_DTYPES
    n = len(UNITS)
    out = pl.pallas_call(
        functools.partial(kernel, STEPS, ARRIVALS, UNITS),
        out_shape=jax.ShapeDtypeStruct((NCODE, OWN, 2, PB, 256), BF16),
        in_specs=[hbm, vmem, smem, smem, smem],
        out_specs=hbm,
        scratch_shapes=[
            vm((NB, PB, W), BF16),
            vm((LOC, PS, W), BF16),
            vm((OWN, 2, 256, PS), BF16),
            vm((n, 256, W), F32),
            vm((SLOTS, 256, W), F32), vm((n, 256, W), F32),
            vm((n, 128, W), rs1), vm((n, 128, W), rs1),
            vm((n, 64, W), rs2), vm((n, 64, W), rs2),
            vm((n, 32, W), rs3), vm((n, 32, W), rs3),
            vm((n, W, W), BF16),
            vm((2, W, W), BF16),
            vm((LOC, PS, W), F32),
            vm((LOC, PS, W), BF16),
            vm((NCODE, LOC, PB, W), BF16),
            vm((2, 2, NCODE, 16, 128), F32),
            vm((1, LOC * W), F32),
            vm((OWN * W, 128), F32),
            dma((2,)), dma((OWN, 2)), dma((1,)), dma((LOC,)),
            dma((n,)), dma((n,)),
            dma((3, n)), dma((3, n)),
            dma((3, n)), dma((3, n)),
            dma((n,)), dma((n,)),
            dma((1,)), dma((LOC,)),
            dma((3,)), dma((3,)),
        ],
        compiler_params=pltpu.CompilerParams(
            collective_id=0, has_side_effects=True, vmem_limit_bytes=62 * 1024 * 1024),
    )(rows, eps_vir.reshape(32, 1, 128), eps_occ, domains.T, pair_keep)
    return jnp.transpose(out.reshape(2 * NB, PB, 256), (1, 0, 2))


def solution(mesh):
    in_specs = (P(("occ", "aux"), None, None), P(), P(), P(), P("occ", None))
    out_specs = P(("occ", "aux"), None, None)
    return jax.shard_map(shards, mesh=mesh, in_specs=in_specs, out_specs=out_specs, check_vma=False)
```

```python
import functools

import jax
import jax.numpy as jnp
from jax import lax
from jax.experimental import pallas as pl
from jax.experimental.pallas import tpu as pltpu
from jax.sharding import PartitionSpec as P

MESH = pl.DeviceIdType.MESH
F32 = jnp.float32
BF16 = jnp.bfloat16

PB = 64
W = 512
NB = 32
OWN = 4
HALO = 3
LOC = OWN + HALO
NCODE = 8
PS = NCODE * PB
SLOTS = 4
ARRIVALS = (4, 1, 3, 0, 2, 5, 6)
UNITS = (
    (3, 3), (3, 1), (4, 2), (6, 3), (5, 0), (4, 3), (5, 3), (5, 1),
    (5, 2), (3, 0), (6, 1), (4, 1), (4, 0), (3, 2), (6, 0), (6, 2),
)
STEPS = (
    (0, 12), (1, 12), (0, 5), (1, 5), (2, 12), (0, 9), (0, 11), (0, 13), (1, 9), (3, 12), (1, 11), (2, 5),
    (1, 13), (0, 0), (4, 12), (1, 0), (2, 9), (2, 11), (3, 5), (2, 13), (5, 12), (0, 1), (0, 2), (1, 1),
    (3, 9), (1, 2), (2, 0), (4, 5), (3, 13), (3, 11), (6, 12), (0, 4), (0, 6), (0, 7), (0, 8), (1, 4),
    (4, 9), (4, 13), (1, 6), (2, 1), (1, 7), (2, 2), (3, 0), (1, 8), (5, 5), (7, 12), (4, 11), (0, 3),
    (0, 10), (5, 9), (8, 12), (1, 3), (5, 13), (0, 14), (3, 1), (1, 10), (0, 15), (4, 0), (2, 4), (2, 6),
    (1, 14), (1, 15), (3, 2), (2, 7), (2, 8), (6, 13), (5, 11), (6, 5), (6, 9), (5, 0), (3, 4), (2, 3),
    (4, 1), (2, 10), (3, 6), (2, 14), (4, 2), (2, 15), (3, 7), (3, 8), (7, 13), (6, 11), (7, 5), (8, 13),
    (6, 0), (8, 5), (3, 3), (4, 6), (7, 9), (3, 10), (5, 2), (4, 4), (5, 1), (8, 9), (3, 15), (4, 8),
    (7, 11), (3, 14), (4, 7), (4, 3), (8, 11), (5, 6), (6, 1), (5, 8), (7, 0), (4, 15), (4, 14), (4, 10),
    (5, 3), (8, 0), (6, 2), (5, 4), (6, 6), (5, 7), (5, 15), (6, 8), (5, 10), (7, 1), (5, 14), (8, 1),
    (7, 2), (6, 3), (7, 6), (8, 2), (6, 4), (8, 6), (6, 7), (6, 14), (6, 15), (7, 8), (7, 3), (8, 8),
    (8, 3), (7, 4), (6, 10), (7, 15), (7, 14), (8, 4), (7, 7), (8, 14), (8, 15), (8, 7), (7, 10), (8, 10),
)
RS_DTYPES = (BF16, BF16, BF16)


def side(pos):
    return lax.rem(lax.div(pos + 1, 2), 2)


def kernel(steps, arrivals, units, b_ref, evir_ref, eocc_ref, dom_ref, keep_ref, out_ref,
           raw, b3, bg, bt, acc, s0, r0, s1, r1, s2, r2, s3, r3, mb, mm, gam, go, rr, kb, erow, ecol,
           loc_sem, out_sem, a_send, a_recv, c_send, c_recv, rs_send, rs_recv, ag_send, ag_recv,
           gc_send, gc_recv, o_send, o_recv, k_send, k_recv):
    occ = lax.axis_index("occ")
    aux = lax.axis_index("aux")
    core = lax.rem(aux, 2)
    pos = (lax.div(occ, 8), lax.div(aux, 2) * 2 + lax.rem(lax.div(occ, 4), 2), lax.rem(occ, 4))
    half = tuple(lax.div(p, 2) for p in pos)
    fs = tuple(side(p) for p in pos)
    code = fs[0] * 4 + fs[1] * 2 + fs[2]

    def device(x, y, z, c):
        return (x * 8 + lax.rem(y, 2) * 4 + z, lax.div(y, 2) * 2 + c)

    group_peers = []
    for r in range(1, 8):
        bits = ((r >> 2) & 1, (r >> 1) & 1, r & 1)
        where = [p + 1 - 2 * lax.rem(p, 2) if bit else p for p, bit in zip(pos, bits)]
        flips = [1 - f if bit else f for f, bit in zip(fs, bits)]
        group_peers.append((device(*where, core), flips[0] * 4 + flips[1] * 2 + flips[2]))
    slice_peers = []
    for d in range(3):
        where = list(pos)
        where[d] = 3 - pos[d]
        slice_peers.append(device(*where, core))
    sibling = device(*pos, 1 - core)

    def remote(src, dst, send, recv, dev):
        return pltpu.make_async_remote_copy(
            src_ref=src, dst_ref=dst, send_sem=send, recv_sem=recv, device_id=dev, device_id_type=MESH)

    load = pltpu.make_async_copy(b_ref, raw, loc_sem.at[0])
    load.start()
    kslot = kb.at[half[2], half[0], code]
    for o in range(2):
        for k in range(LOC):
            kslot[o * LOC + k:o * LOC + k + 1, :] = jnp.full((1, 128), keep_ref[o, k].astype(F32))

    barrier = pltpu.get_barrier_semaphore()
    everyone = [dev for dev, _ in group_peers] + slice_peers + [sibling]
    for dev in everyone:
        pl.semaphore_signal(barrier, inc=1, device_id=dev, device_id_type=MESH)
    load.wait()

    def turn(m, _):
        for p in range(0, PB, 32):
            part = raw[p:p + 32, pl.ds(pl.multiple_of(m * 16, 16), 16), :].astype(F32)
            part = jnp.swapaxes(part, 0, 1).astype(BF16)
            for i in range(16):
                b3[m * 8 + i // 2, p:p + 32, i % 2 * 256:i % 2 * 256 + 256] = part[i]
        return 0

    lax.fori_loop(0, 4, turn, 0)
    pl.semaphore_wait(barrier, len(everyone))

    first = code * OWN - HALO + NB

    def send_in(t):
        for dev, q in group_peers:
            batch = lax.rem(q * OWN - HALO + NB + t, NB)
            remote(b3.at[batch], bg.at[t, pl.ds(pl.multiple_of(code * PB, PB), PB)], a_send.at[0], a_recv.at[t], dev).start()

    for dev, q in group_peers:
        remote(kslot, kslot, k_send.at[0], k_recv.at[0], dev).start()
    for t in arrivals:
        send_in(t)

    def own_rows(t, _):
        batch = lax.rem(first + t, NB)
        bg[t, pl.ds(pl.multiple_of(code * PB, PB), PB), :] = b3[batch]
        return 0

    lax.fori_loop(0, LOC, own_rows, 0)

    for t in range(LOC):
        for o in range(2):
            orb = lax.rem(first + t, NB) * 2 + o
            for k in range(2):
                row = evir_ref[dom_ref[k, orb]] - eocc_ref[orb]
                lane = t * W + o * 256 + k * 128
                erow[:, lane:lane + 128] = row
                if t >= HALO:
                    at = lane - HALO * W
                    ecol[at:at + 128, :] = jnp.broadcast_to(row, (128, 128)).T

    def keep_group():
        pltpu.make_async_copy(kb.at[0, 0, pl.ds(0, 7)], kb.at[0, 0, pl.ds(0, 7)], k_recv.at[0]).wait()
        pltpu.make_async_copy(kb.at[0, 0, pl.ds(0, 7)], kb.at[0, 0, pl.ds(0, 7)], k_send.at[0]).wait()

    def keep_x():
        ref = kb.at[half[2], half[0]]
        return remote(ref, ref, k_send.at[1], k_recv.at[1], slice_peers[0])

    def keep_z():
        ref = kb.at[half[2]]
        return remote(ref, ref, k_send.at[2], k_recv.at[2], slice_peers[2])

    def order(u, n):
        return (u + n) % 3

    def wait_in(t):
        pltpu.make_async_copy(bg.at[0, pl.ds(0, 7 * PB)], bg.at[0, pl.ds(0, 7 * PB)], a_recv.at[t]).wait()

    arrived, turned, touched = set(), set(), set()
    started = []
    left = [0] * LOC
    for top, s in units:
        left[top] += 1
        if s:
            left[top - s] += 1

    def core_copy(u):
        return remote(s0.at[started.index(u) % SLOTS], r0.at[u], c_send.at[u], c_recv.at[u], sibling)

    rs_bufs = ((s1, r1), (s2, r2), (s3, r3))

    def rs_copy(n, u):
        sb, rb = rs_bufs[n]
        return remote(sb.at[u], rb.at[u], rs_send.at[n, u], rs_recv.at[n, u], slice_peers[order(u, n)])

    def base_rows(u, n):
        at = core * 0
        for m in range(n):
            at = at + half[order(u, m)] * (128 >> m)
        return at

    def ag_copy(n, u):
        size = 128 >> n
        ref = mb.at[u, pl.ds(pl.multiple_of(core * 256 + base_rows(u, n + 1), 32), size)]
        return remote(ref, ref, ag_send.at[n, u], ag_recv.at[n, u], slice_peers[order(u, n)])

    def gc_copy(u):
        ref = mb.at[u, pl.ds(pl.multiple_of(core * 256, 256), 256)]
        return remote(ref, ref, gc_send.at[u], gc_recv.at[u], sibling)

    def stage_v(u):
        top, s = units[u]
        for t in (top, top - s):
            if t not in arrived:
                wait_in(t)
                arrived.add(t)
        own = top - HALO
        if top not in turned:
            turned.add(top)
            for h in range(2):
                lanes = core * 256 if h == 0 else (1 - core) * 256
                bt[own, h] = bg[top, :, pl.ds(pl.multiple_of(lanes, 256), 256)].T
        if len(started) >= SLOTS:
            core_copy(started[-SLOTS]).wait_send()
        started.append(u)
        other = bg[top - s]
        s0[started.index(u) % SLOTS] = jnp.dot(bt[own, 1], other, preferred_element_type=F32)
        core_copy(u).start()
        acc[u] = jnp.dot(bt[own, 0], other, preferred_element_type=F32)

    def fold(n, u):
        src = r0 if n == 0 else rs_bufs[n - 1][1]
        if n == 0:
            core_copy(u).wait_recv()
        else:
            rs_copy(n - 1, u).wait_recv()
        size = 128 >> n
        near_half = half[order(u, n)]
        base = base_rows(u, n)
        keep_at = near_half * size
        send_at = (1 - near_half) * size
        send_to = rs_bufs[n][0]
        step = 32

        def far(k, _):
            near = pl.ds(pl.multiple_of(send_at + k * step, step), step)
            mine = pl.ds(pl.multiple_of(base + send_at + k * step, step), step)
            val = acc[u, mine, :] + src[u, near, :].astype(F32)
            send_to[u, pl.ds(pl.multiple_of(k * step, step), step), :] = val.astype(send_to.dtype)
            return 0

        lax.fori_loop(0, size // step, far, 0)
        rs_copy(n, u).start()

        def stay(k, _):
            near = pl.ds(pl.multiple_of(keep_at + k * step, step), step)
            mine = pl.ds(pl.multiple_of(base + keep_at + k * step, step), step)
            acc[u, mine, :] = acc[u, mine, :] + src[u, near, :].astype(F32)
            return 0

        lax.fori_loop(0, size // step, stay, 0)

    def stage_amp(u):
        rs_copy(2, u).wait_recv()
        top, s = units[u]
        base = pl.multiple_of(base_rows(u, 3), 32)
        rows = ecol[pl.ds(pl.multiple_of((top - HALO) * W + core * 256 + base, 32), 32), :]
        for k in range(W // 128):
            lanes = slice(k * 128, k * 128 + 128)
            at = (top - s) * W + k * 128
            total = acc[u, pl.ds(base, 32), lanes] + r3[u, :, lanes]
            denom = rows + erow[:, at:at + 128]
            mb[u, pl.ds(pl.multiple_of(core * 256 + base, 32), 32), lanes] = (-total / denom).astype(BF16)
        ag_copy(2, u).start()

    def stage_ag(n, u):
        ag_copy(n + 1, u).wait_recv()
        ag_copy(n, u).start()

    def stage_gc(u):
        ag_copy(0, u).wait_recv()
        gc_copy(u).start()

    def flag(t, orbital, offset):
        batch = lax.rem(first + t, NB)
        y = half[1] * 2 + lax.rem(lax.div(batch, 4), 2)
        x, z = lax.div(batch, 8), lax.rem(batch, 4)
        q = side(x) * 4 + side(y) * 2 + side(z)
        row = orbital * LOC + offset
        line = kb[lax.div(z, 2), lax.div(x, 2), q, row:row + 1, :]
        return jnp.broadcast_to(line, (256, 128)).astype(BF16)

    finished = []

    def finish(t):
        finished.append(t)
        go[t] = gam[t].astype(BF16)
        for dev, q in group_peers:
            remote(go.at[t, pl.ds(pl.multiple_of(q * PB, PB), PB)], rr.at[code, t], o_send.at[0], o_recv.at[t], dev).start()
        rr[code, t] = go[t, pl.ds(pl.multiple_of(code * PB, PB), PB)]

    def add_term(t, part):
        if t in touched:
            gam[t] = gam[t] + part
        else:
            touched.add(t)
            gam[t] = part
        left[t] -= 1
        if left[t] == 0:
            finish(t)

    def stage_gamma(u):
        top, s = units[u]
        gc_copy(u).wait_recv()
        if s:
            for o in range(2):
                m = flag(top - s, o, HALO - s)
                for k in range(2):
                    lanes = slice(o * 256 + k * 128, o * 256 + k * 128 + 128)
                    for h in range(2):
                        mm[0, h * 256:h * 256 + 256, lanes] = mb[u, h * 256:h * 256 + 256, lanes] * m
            add_term(top - s, jnp.dot(bg[top], mm[0], preferred_element_type=F32))
        for h in range(2):
            m = flag(top, h, HALO + s)
            for k in range(4):
                lanes = slice(k * 128, k * 128 + 128)
                mm[1, h * 256:h * 256 + 256, lanes] = mb[u, h * 256:h * 256 + 256, lanes] * m
        add_term(top, lax.dot_general(bg[top - s], mm[1], (((1,), (1,)), ((), ())), preferred_element_type=F32))

    stages = [
        stage_v,
        lambda u: fold(0, u),
        lambda u: fold(1, u),
        lambda u: fold(2, u),
        stage_amp,
        lambda u: stage_ag(1, u),
        lambda u: stage_ag(0, u),
        stage_gc,
        stage_gamma,
    ]
    seen = set()
    for stage, u in steps:
        if stage not in seen:
            if stage == 1:
                keep_group()
                keep_x().start()
            if stage == 4:
                keep_x().wait()
                keep_z().start()
            if stage == 8:
                keep_z().wait()
        seen.add(stage)
        stages[stage](u)

    pltpu.make_async_copy(rr.at[pl.ds(0, 7)], rr.at[pl.ds(0, 7)], a_send.at[0]).wait()
    for at, u in enumerate(started):
        if at >= len(started) - SLOTS:
            core_copy(u).wait_send()
        gc_copy(u).wait_send()
        for n in range(3):
            rs_copy(n, u).wait_send()
            ag_copy(n, u).wait_send()

    got, done = set(), set()
    stores = []
    for t in finished:
        pltpu.make_async_copy(bg.at[0, pl.ds(0, 7 * PB)], bg.at[0, pl.ds(0, 7 * PB)], o_recv.at[t]).wait()
        got.add(t)
        for k in range(OWN):
            if k in done or HALO + k not in got or (k and k - 1 not in got):
                continue
            done.add(k)
            if k:
                def combine(g, _, k=k):
                    nxt = lax.rem(g + 1, NCODE)
                    rr[g, HALO + k] = (rr[g, HALO + k].astype(F32) + rr[nxt, k - 1].astype(F32)).astype(BF16)
                    return 0

                lax.fori_loop(0, NCODE, combine, 0)
            for o in range(2):
                cp = pltpu.make_async_copy(rr.at[:, HALO + k, :, pl.ds(o * 256, 256)], out_ref.at[:, k, o], out_sem.at[k, o])
                cp.start()
                stores.append(cp)
    for cp in stores:
        cp.wait()
    pltpu.make_async_copy(rr.at[pl.ds(0, 7)], rr.at[pl.ds(0, 7)], o_send.at[0]).wait()


def shards(b_aux, eps_occ, eps_vir, domains, pair_keep):
    dma, vm = pltpu.SemaphoreType.DMA, pltpu.VMEM
    hbm = pl.BlockSpec(memory_space=pl.ANY)
    vmem = pl.BlockSpec(memory_space=pltpu.VMEM)
    smem = pl.BlockSpec(memory_space=pltpu.SMEM)
    rs1, rs2, rs3 = RS_DTYPES
    n = len(UNITS)
    out = pl.pallas_call(
        functools.partial(kernel, STEPS, ARRIVALS, UNITS),
        out_shape=jax.ShapeDtypeStruct((NCODE, OWN, 2, PB, 256), BF16),
        in_specs=[hbm, vmem, smem, smem, smem],
        out_specs=hbm,
        scratch_shapes=[
            vm((PB, 2 * NB, 256), BF16),
            vm((NB, PB, W), BF16),
            vm((LOC, PS, W), BF16),
            vm((OWN, 2, 256, PS), BF16),
            vm((n, 256, W), F32),
            vm((SLOTS, 256, W), F32), vm((n, 256, W), F32),
            vm((n, 128, W), rs1), vm((n, 128, W), rs1),
            vm((n, 64, W), rs2), vm((n, 64, W), rs2),
            vm((n, 32, W), rs3), vm((n, 32, W), rs3),
            vm((n, W, W), BF16),
            vm((2, W, W), BF16),
            vm((LOC, PS, W), F32),
            vm((LOC, PS, W), BF16),
            vm((NCODE, LOC, PB, W), BF16),
            vm((2, 2, NCODE, 16, 128), F32),
            vm((1, LOC * W), F32),
            vm((OWN * W, 128), F32),
            dma((2,)), dma((OWN, 2)), dma((1,)), dma((LOC,)),
            dma((n,)), dma((n,)),
            dma((3, n)), dma((3, n)),
            dma((3, n)), dma((3, n)),
            dma((n,)), dma((n,)),
            dma((1,)), dma((LOC,)),
            dma((3,)), dma((3,)),
        ],
        compiler_params=pltpu.CompilerParams(
            collective_id=0, has_side_effects=True, vmem_limit_bytes=62 * 1024 * 1024),
    )(b_aux, eps_vir.reshape(32, 1, 128), eps_occ, domains.T, pair_keep)
    return jnp.transpose(out.reshape(2 * NB, PB, 256), (1, 0, 2))


def solution(mesh):
    in_specs = (P(("occ", "aux"), None, None), P(), P(), P(), P("occ", None))
    out_specs = P(("occ", "aux"), None, None)
    return jax.shard_map(shards, mesh=mesh, in_specs=in_specs, out_specs=out_specs, check_vma=False)
```

```python
import functools

import jax
import jax.numpy as jnp
from jax import lax
from jax.experimental import pallas as pl
from jax.experimental.pallas import tpu as pltpu
from jax.sharding import PartitionSpec as P

MESH = pl.DeviceIdType.MESH
F32 = jnp.float32
BF16 = jnp.bfloat16

PB = 64
W = 512
NB = 32
OWN = 4
HALO = 3
LOC = OWN + HALO
NCODE = 8
PS = NCODE * PB
SLOTS = 4
ARRIVALS = (1, 4, 3, 5, 2, 0, 6)
UNITS = (
    (3, 0), (5, 1), (6, 0), (3, 1), (3, 2), (5, 3), (6, 3), (6, 1),
    (5, 2), (4, 3), (3, 3), (4, 1), (5, 0), (4, 2), (4, 0), (6, 2),
)
STEPS = (
    (0, 14), (1, 14), (0, 4), (0, 11), (0, 9), (1, 4), (0, 0), (1, 0), (2, 14), (1, 9), (0, 1), (2, 4),
    (1, 11), (0, 12), (1, 12), (0, 8), (2, 0), (1, 1), (0, 3), (2, 9), (1, 8), (3, 14), (0, 13), (0, 5),
    (2, 11), (3, 4), (1, 3), (2, 12), (1, 13), (0, 10), (3, 9), (2, 1), (3, 11), (1, 10), (2, 8), (1, 5),
    (2, 3), (4, 9), (4, 4), (3, 1), (0, 6), (2, 13), (4, 14), (4, 11), (0, 7), (2, 10), (1, 6), (0, 2),
    (3, 8), (3, 3), (1, 7), (3, 0), (0, 15), (5, 4), (2, 5), (3, 13), (3, 10), (5, 9), (1, 2), (1, 15),
    (4, 0), (2, 6), (4, 8), (4, 13), (4, 10), (3, 5), (4, 3), (6, 9), (3, 12), (2, 7), (6, 4), (5, 10),
    (2, 15), (5, 8), (4, 1), (4, 5), (7, 9), (3, 6), (5, 3), (5, 13), (3, 7), (2, 2), (4, 12), (8, 9),
    (7, 4), (6, 10), (5, 11), (4, 6), (6, 8), (5, 0), (8, 4), (5, 5), (5, 1), (6, 13), (7, 10), (3, 15),
    (6, 3), (5, 6), (4, 7), (7, 8), (6, 5), (6, 11), (6, 0), (5, 14), (8, 10), (7, 13), (5, 12), (6, 6),
    (7, 3), (8, 13), (6, 1), (7, 5), (3, 2), (4, 15), (8, 3), (5, 7), (8, 5), (8, 8), (7, 0), (7, 6),
    (6, 12), (6, 14), (5, 15), (7, 1), (7, 11), (8, 0), (6, 7), (8, 6), (8, 11), (8, 1), (6, 15), (7, 12),
    (4, 2), (7, 7), (7, 14), (8, 12), (8, 7), (7, 15), (5, 2), (8, 15), (6, 2), (8, 14), (7, 2), (8, 2),
)
RS_DTYPES = (BF16, BF16, BF16)


def side(pos):
    return lax.rem(lax.div(pos + 1, 2), 2)


def kernel(steps, arrivals, units, b_ref, evir_ref, eocc_ref, dom_ref, keep_ref, out_ref,
           raw, b3, bg, bt, acc, s0, r0, s1, r1, s2, r2, s3, r3, mb, mm, gam, go, rr, kb, erow, ecol,
           loc_sem, out_sem, a_send, a_recv, c_send, c_recv, rs_send, rs_recv, ag_send, ag_recv,
           gc_send, gc_recv, o_send, o_recv, k_send, k_recv):
    occ = lax.axis_index("occ")
    aux = lax.axis_index("aux")
    core = lax.rem(aux, 2)
    pos = (lax.div(occ, 8), lax.div(aux, 2) * 2 + lax.rem(lax.div(occ, 4), 2), lax.rem(occ, 4))
    half = tuple(lax.div(p, 2) for p in pos)
    fs = tuple(side(p) for p in pos)
    code = fs[0] * 4 + fs[1] * 2 + fs[2]

    def device(x, y, z, c):
        return (x * 8 + lax.rem(y, 2) * 4 + z, lax.div(y, 2) * 2 + c)

    group_peers = []
    for r in range(1, 8):
        bits = ((r >> 2) & 1, (r >> 1) & 1, r & 1)
        where = [p + 1 - 2 * lax.rem(p, 2) if bit else p for p, bit in zip(pos, bits)]
        flips = [1 - f if bit else f for f, bit in zip(fs, bits)]
        group_peers.append((device(*where, core), flips[0] * 4 + flips[1] * 2 + flips[2]))
    slice_peers = []
    for d in range(3):
        where = list(pos)
        where[d] = 3 - pos[d]
        slice_peers.append(device(*where, core))
    sibling = device(*pos, 1 - core)

    def remote(src, dst, send, recv, dev):
        return pltpu.make_async_remote_copy(
            src_ref=src, dst_ref=dst, send_sem=send, recv_sem=recv, device_id=dev, device_id_type=MESH)

    load = pltpu.make_async_copy(b_ref, raw, loc_sem.at[0])
    load.start()
    kslot = kb.at[half[2], half[0], code]
    for o in range(2):
        for k in range(LOC):
            kslot[o * LOC + k:o * LOC + k + 1, :] = jnp.full((1, 128), keep_ref[o, k].astype(F32))

    barrier = pltpu.get_barrier_semaphore()
    everyone = [dev for dev, _ in group_peers] + slice_peers + [sibling]
    for dev in everyone:
        pl.semaphore_signal(barrier, inc=1, device_id=dev, device_id_type=MESH)
    load.wait()

    def turn(m, _):
        for p in range(0, PB, 32):
            part = raw[p:p + 32, pl.ds(pl.multiple_of(m * 16, 16), 16), :].astype(F32)
            part = jnp.swapaxes(part, 0, 1).astype(BF16)
            for i in range(16):
                b3[m * 8 + i // 2, p:p + 32, i % 2 * 256:i % 2 * 256 + 256] = part[i]
        return 0

    lax.fori_loop(0, 4, turn, 0)
    pl.semaphore_wait(barrier, len(everyone))

    first = code * OWN - HALO + NB

    def send_in(t):
        for dev, q in group_peers:
            batch = lax.rem(q * OWN - HALO + NB + t, NB)
            remote(b3.at[batch], bg.at[t, pl.ds(pl.multiple_of(code * PB, PB), PB)], a_send.at[0], a_recv.at[t], dev).start()

    for dev, q in group_peers:
        remote(kslot, kslot, k_send.at[0], k_recv.at[0], dev).start()
    for t in arrivals:
        send_in(t)

    def own_rows(t, _):
        batch = lax.rem(first + t, NB)
        bg[t, pl.ds(pl.multiple_of(code * PB, PB), PB), :] = b3[batch]
        return 0

    lax.fori_loop(0, LOC, own_rows, 0)

    for t in range(LOC):
        for o in range(2):
            orb = lax.rem(first + t, NB) * 2 + o
            for k in range(2):
                row = evir_ref[dom_ref[k, orb]] - eocc_ref[orb]
                lane = t * W + o * 256 + k * 128
                erow[:, lane:lane + 128] = row
                if t >= HALO:
                    at = lane - HALO * W
                    ecol[at:at + 128, :] = jnp.broadcast_to(row, (128, 128)).T

    def keep_group():
        pltpu.make_async_copy(kb.at[0, 0, pl.ds(0, 7)], kb.at[0, 0, pl.ds(0, 7)], k_recv.at[0]).wait()
        pltpu.make_async_copy(kb.at[0, 0, pl.ds(0, 7)], kb.at[0, 0, pl.ds(0, 7)], k_send.at[0]).wait()

    def keep_x():
        ref = kb.at[half[2], half[0]]
        return remote(ref, ref, k_send.at[1], k_recv.at[1], slice_peers[0])

    def keep_z():
        ref = kb.at[half[2]]
        return remote(ref, ref, k_send.at[2], k_recv.at[2], slice_peers[2])

    def order(u, n, h):
        return (u + n + h) % 3

    def cols(h):
        return pl.ds(h * 256, 256)

    def wait_in(t):
        pltpu.make_async_copy(bg.at[0, pl.ds(0, 7 * PB)], bg.at[0, pl.ds(0, 7 * PB)], a_recv.at[t]).wait()

    arrived, turned, touched = set(), set(), set()
    started = []
    left = [0] * LOC
    for top, s in units:
        left[top] += 1
        if s:
            left[top - s] += 1

    def core_copy(u):
        return remote(s0.at[started.index(u) % SLOTS], r0.at[u], c_send.at[u], c_recv.at[u], sibling)

    rs_bufs = ((s1, r1), (s2, r2), (s3, r3))

    def rs_copy(n, u, h):
        sb, rb = rs_bufs[n]
        return remote(sb.at[u, :, cols(h)], rb.at[u, :, cols(h)], rs_send.at[n, u, h], rs_recv.at[n, u, h],
                      slice_peers[order(u, n, h)])

    def base_rows(u, n, h):
        at = core * 0
        for m in range(n):
            at = at + half[order(u, m, h)] * (128 >> m)
        return at

    def ag_copy(n, u, h):
        size = 128 >> n
        ref = mb.at[u, pl.ds(pl.multiple_of(core * 256 + base_rows(u, n + 1, h), 32), size), cols(h)]
        return remote(ref, ref, ag_send.at[n, u, h], ag_recv.at[n, u, h], slice_peers[order(u, n, h)])

    def gc_copy(u):
        ref = mb.at[u, pl.ds(pl.multiple_of(core * 256, 256), 256)]
        return remote(ref, ref, gc_send.at[u], gc_recv.at[u], sibling)

    def stage_v(u):
        top, s = units[u]
        for t in (top, top - s):
            if t not in arrived:
                wait_in(t)
                arrived.add(t)
        own = top - HALO
        if top not in turned:
            turned.add(top)
            for h in range(2):
                lanes = core * 256 if h == 0 else (1 - core) * 256
                bt[own, h] = bg[top, :, pl.ds(pl.multiple_of(lanes, 256), 256)].T
        if len(started) >= SLOTS:
            core_copy(started[-SLOTS]).wait_send()
        started.append(u)
        other = bg[top - s]
        s0[started.index(u) % SLOTS] = jnp.dot(bt[own, 1], other, preferred_element_type=F32)
        core_copy(u).start()
        acc[u] = jnp.dot(bt[own, 0], other, preferred_element_type=F32)

    def fold(n, u):
        src = r0 if n == 0 else rs_bufs[n - 1][1]
        size = 128 >> n
        send_to = rs_bufs[n][0]
        step = 32
        if n == 0:
            core_copy(u).wait_recv()
        for h in range(2):
            if n:
                rs_copy(n - 1, u, h).wait_recv()
            lanes = slice(h * 256, h * 256 + 256)
            base = base_rows(u, n, h)
            send_at = (1 - half[order(u, n, h)]) * size

            def far(k, _):
                near = pl.ds(pl.multiple_of(send_at + k * step, step), step)
                mine = pl.ds(pl.multiple_of(base + send_at + k * step, step), step)
                val = acc[u, mine, lanes] + src[u, near, lanes].astype(F32)
                send_to[u, pl.ds(pl.multiple_of(k * step, step), step), lanes] = val.astype(send_to.dtype)
                return 0

            lax.fori_loop(0, size // step, far, 0)
            rs_copy(n, u, h).start()
        for h in range(2):
            lanes = slice(h * 256, h * 256 + 256)
            base = base_rows(u, n, h)
            keep_at = half[order(u, n, h)] * size

            def stay(k, _):
                near = pl.ds(pl.multiple_of(keep_at + k * step, step), step)
                mine = pl.ds(pl.multiple_of(base + keep_at + k * step, step), step)
                acc[u, mine, lanes] = acc[u, mine, lanes] + src[u, near, lanes].astype(F32)
                return 0

            lax.fori_loop(0, size // step, stay, 0)

    def stage_amp(u):
        top, s = units[u]
        for h in range(2):
            rs_copy(2, u, h).wait_recv()
            base = pl.multiple_of(base_rows(u, 3, h), 32)
            rows = ecol[pl.ds(pl.multiple_of((top - HALO) * W + core * 256 + base, 32), 32), :]
            for k in range(2 * h, 2 * h + 2):
                lanes = slice(k * 128, k * 128 + 128)
                at = (top - s) * W + k * 128
                total = acc[u, pl.ds(base, 32), lanes] + r3[u, :, lanes].astype(F32)
                denom = rows + erow[:, at:at + 128]
                mb[u, pl.ds(pl.multiple_of(core * 256 + base, 32), 32), lanes] = (-total / denom).astype(BF16)
            ag_copy(2, u, h).start()

    def stage_ag(n, u):
        for h in range(2):
            ag_copy(n + 1, u, h).wait_recv()
            ag_copy(n, u, h).start()

    def stage_gc(u):
        for h in range(2):
            ag_copy(0, u, h).wait_recv()
        gc_copy(u).start()

    def flag(t, orbital, offset):
        batch = lax.rem(first + t, NB)
        y = half[1] * 2 + lax.rem(lax.div(batch, 4), 2)
        x, z = lax.div(batch, 8), lax.rem(batch, 4)
        q = side(x) * 4 + side(y) * 2 + side(z)
        row = orbital * LOC + offset
        line = kb[lax.div(z, 2), lax.div(x, 2), q, row:row + 1, :]
        return jnp.broadcast_to(line, (256, 128)).astype(BF16)

    finished = []

    def finish(t):
        finished.append(t)
        go[t] = gam[t].astype(BF16)
        for dev, q in group_peers:
            remote(go.at[t, pl.ds(pl.multiple_of(q * PB, PB), PB)], rr.at[code, t], o_send.at[0], o_recv.at[t], dev).start()
        rr[code, t] = go[t, pl.ds(pl.multiple_of(code * PB, PB), PB)]

    def add_term(t, part):
        if t in touched:
            gam[t] = gam[t] + part
        else:
            touched.add(t)
            gam[t] = part
        left[t] -= 1
        if left[t] == 0:
            finish(t)

    def stage_gamma(u):
        top, s = units[u]
        gc_copy(u).wait_recv()
        if s:
            for o in range(2):
                m = flag(top - s, o, HALO - s)
                for k in range(2):
                    lanes = slice(o * 256 + k * 128, o * 256 + k * 128 + 128)
                    for h in range(2):
                        mm[0, h * 256:h * 256 + 256, lanes] = mb[u, h * 256:h * 256 + 256, lanes] * m
            add_term(top - s, jnp.dot(bg[top], mm[0], preferred_element_type=F32))
        for h in range(2):
            m = flag(top, h, HALO + s)
            for k in range(4):
                lanes = slice(k * 128, k * 128 + 128)
                mm[1, h * 256:h * 256 + 256, lanes] = mb[u, h * 256:h * 256 + 256, lanes] * m
        add_term(top, lax.dot_general(bg[top - s], mm[1], (((1,), (1,)), ((), ())), preferred_element_type=F32))

    stages = [
        stage_v,
        lambda u: fold(0, u),
        lambda u: fold(1, u),
        lambda u: fold(2, u),
        stage_amp,
        lambda u: stage_ag(1, u),
        lambda u: stage_ag(0, u),
        stage_gc,
        stage_gamma,
    ]
    seen = set()
    for stage, u in steps:
        if stage not in seen:
            if stage == 1:
                keep_group()
                keep_x().start()
            if stage == 4:
                keep_x().wait()
                keep_z().start()
            if stage == 8:
                keep_z().wait()
        seen.add(stage)
        stages[stage](u)

    pltpu.make_async_copy(rr.at[pl.ds(0, 7)], rr.at[pl.ds(0, 7)], a_send.at[0]).wait()
    for at, u in enumerate(started):
        if at >= len(started) - SLOTS:
            core_copy(u).wait_send()
        gc_copy(u).wait_send()
        for n in range(3):
            for h in range(2):
                rs_copy(n, u, h).wait_send()
                ag_copy(n, u, h).wait_send()

    got, done = set(), set()
    stores = []
    for t in finished:
        pltpu.make_async_copy(bg.at[0, pl.ds(0, 7 * PB)], bg.at[0, pl.ds(0, 7 * PB)], o_recv.at[t]).wait()
        got.add(t)
        for k in range(OWN):
            if k in done or HALO + k not in got or (k and k - 1 not in got):
                continue
            done.add(k)
            if k:
                def combine(g, _, k=k):
                    nxt = lax.rem(g + 1, NCODE)
                    rr[g, HALO + k] = (rr[g, HALO + k].astype(F32) + rr[nxt, k - 1].astype(F32)).astype(BF16)
                    return 0

                lax.fori_loop(0, NCODE, combine, 0)
            for o in range(2):
                cp = pltpu.make_async_copy(rr.at[:, HALO + k, :, pl.ds(o * 256, 256)], out_ref.at[:, k, o], out_sem.at[k, o])
                cp.start()
                stores.append(cp)
    for cp in stores:
        cp.wait()
    pltpu.make_async_copy(rr.at[pl.ds(0, 7)], rr.at[pl.ds(0, 7)], o_send.at[0]).wait()


def shards(b_aux, eps_occ, eps_vir, domains, pair_keep):
    dma, vm = pltpu.SemaphoreType.DMA, pltpu.VMEM
    hbm = pl.BlockSpec(memory_space=pl.ANY)
    vmem = pl.BlockSpec(memory_space=pltpu.VMEM)
    smem = pl.BlockSpec(memory_space=pltpu.SMEM)
    rs1, rs2, rs3 = RS_DTYPES
    n = len(UNITS)
    out = pl.pallas_call(
        functools.partial(kernel, STEPS, ARRIVALS, UNITS),
        out_shape=jax.ShapeDtypeStruct((NCODE, OWN, 2, PB, 256), BF16),
        in_specs=[hbm, vmem, smem, smem, smem],
        out_specs=hbm,
        scratch_shapes=[
            vm((PB, 2 * NB, 256), BF16),
            vm((NB, PB, W), BF16),
            vm((LOC, PS, W), BF16),
            vm((OWN, 2, 256, PS), BF16),
            vm((n, 256, W), F32),
            vm((SLOTS, 256, W), F32), vm((n, 256, W), F32),
            vm((n, 128, W), rs1), vm((n, 128, W), rs1),
            vm((n, 64, W), rs2), vm((n, 64, W), rs2),
            vm((n, 32, W), rs3), vm((n, 32, W), rs3),
            vm((n, W, W), BF16),
            vm((2, W, W), BF16),
            vm((LOC, PS, W), F32),
            vm((LOC, PS, W), BF16),
            vm((NCODE, LOC, PB, W), BF16),
            vm((2, 2, NCODE, 16, 128), F32),
            vm((1, LOC * W), F32),
            vm((OWN * W, 128), F32),
            dma((2,)), dma((OWN, 2)), dma((1,)), dma((LOC,)),
            dma((n,)), dma((n,)),
            dma((3, n, 2)), dma((3, n, 2)),
            dma((3, n, 2)), dma((3, n, 2)),
            dma((n,)), dma((n,)),
            dma((1,)), dma((LOC,)),
            dma((3,)), dma((3,)),
        ],
        compiler_params=pltpu.CompilerParams(
            collective_id=0, has_side_effects=True, vmem_limit_bytes=62 * 1024 * 1024),
    )(b_aux, eps_vir.reshape(32, 1, 128), eps_occ, domains.T, pair_keep)
    return jnp.transpose(out.reshape(2 * NB, PB, 256), (1, 0, 2))


def solution(mesh):
    in_specs = (P(("occ", "aux"), None, None), P(), P(), P(), P("occ", None))
    out_specs = P(("occ", "aux"), None, None)
    return jax.shard_map(shards, mesh=mesh, in_specs=in_specs, out_specs=out_specs, check_vma=False)
```

```python
import functools

import jax
import jax.numpy as jnp
from jax import lax
from jax.experimental import pallas as pl
from jax.experimental.pallas import tpu as pltpu
from jax.sharding import PartitionSpec as P

MESH = pl.DeviceIdType.MESH
F32 = jnp.float32
BF16 = jnp.bfloat16

PB = 64
W = 512
NB = 32
OWN = 4
HALO = 3
LOC = OWN + HALO
NCODE = 8
PS = NCODE * PB
SLOTS = 4
ARRIVALS = (3, 1, 4, 0, 6, 5, 2)
UNITS = (
    (6, 1), (6, 2), (3, 0), (4, 2), (4, 3), (3, 2), (4, 0), (5, 1),
    (6, 3), (5, 3), (6, 0), (3, 1), (4, 1), (3, 3), (5, 2), (5, 0),
)
STEPS = (
    (0, 2), (1, 2), (0, 5), (2, 2), (1, 5), (0, 4), (3, 2), (0, 6), (0, 12), (2, 5), (1, 4), (1, 6),
    (1, 12), (4, 2), (0, 13), (3, 5), (1, 13), (2, 4), (2, 6), (2, 12), (5, 2), (4, 5), (0, 1), (0, 8),
    (0, 10), (2, 13), (1, 1), (3, 4), (1, 8), (3, 6), (1, 10), (3, 12), (6, 2), (5, 5), (0, 0), (3, 13),
    (0, 7), (4, 4), (2, 1), (1, 0), (1, 7), (2, 8), (4, 6), (6, 5), (2, 10), (4, 12), (4, 13), (5, 4),
    (7, 2), (0, 3), (3, 1), (2, 0), (8, 2), (1, 3), (2, 7), (5, 6), (3, 8), (7, 5), (0, 9), (3, 10),
    (6, 4), (5, 12), (5, 13), (8, 5), (3, 0), (4, 1), (1, 9), (2, 3), (6, 6), (3, 7), (4, 8), (4, 10),
    (7, 4), (0, 11), (6, 12), (5, 1), (6, 13), (8, 4), (4, 0), (1, 11), (2, 9), (3, 3), (7, 6), (0, 14),
    (4, 7), (5, 8), (5, 10), (8, 6), (5, 0), (6, 1), (1, 14), (7, 12), (0, 15), (2, 11), (8, 12), (4, 3),
    (3, 9), (7, 13), (1, 15), (5, 7), (6, 10), (6, 8), (8, 13), (6, 0), (7, 1), (3, 11), (2, 14), (5, 3),
    (8, 1), (4, 9), (2, 15), (6, 7), (7, 10), (8, 10), (7, 0), (7, 8), (4, 11), (3, 14), (5, 9), (6, 3),
    (8, 0), (3, 15), (8, 8), (7, 7), (5, 11), (4, 14), (6, 9), (8, 7), (4, 15), (7, 3), (6, 11), (8, 3),
    (5, 14), (7, 9), (5, 15), (8, 9), (7, 11), (6, 14), (8, 11), (6, 15), (7, 14), (8, 14), (7, 15), (8, 15),
)
RS_DTYPES = (BF16, BF16, BF16)


def side(pos):
    return lax.rem(lax.div(pos + 1, 2), 2)


def kernel(steps, arrivals, units, b_ref, evir_ref, eocc_ref, dom_ref, keep_ref, out_ref,
           raw, b3, bg, bt, acc, s0, r0, s1, r1, s2, r2, s3, r3, mb, mm, gam, go, rr, kb, erow, ecol,
           loc_sem, out_sem, a_send, a_recv, c_send, c_recv, rs_send, rs_recv, ag_send, ag_recv,
           gc_send, gc_recv, o_send, o_recv, k_send, k_recv):
    occ = lax.axis_index("occ")
    aux = lax.axis_index("aux")
    core = lax.rem(aux, 2)
    pos = (lax.div(occ, 8), lax.div(aux, 2) * 2 + lax.rem(lax.div(occ, 4), 2), lax.rem(occ, 4))
    half = tuple(lax.div(p, 2) for p in pos)
    fs = tuple(side(p) for p in pos)
    code = fs[0] * 4 + fs[1] * 2 + fs[2]

    def device(x, y, z, c):
        return (x * 8 + lax.rem(y, 2) * 4 + z, lax.div(y, 2) * 2 + c)

    group_peers = []
    for r in range(1, 8):
        bits = ((r >> 2) & 1, (r >> 1) & 1, r & 1)
        where = [p + 1 - 2 * lax.rem(p, 2) if bit else p for p, bit in zip(pos, bits)]
        flips = [1 - f if bit else f for f, bit in zip(fs, bits)]
        group_peers.append((device(*where, core), flips[0] * 4 + flips[1] * 2 + flips[2]))
    slice_peers = []
    for d in range(3):
        where = list(pos)
        where[d] = 3 - pos[d]
        slice_peers.append(device(*where, core))
    sibling = device(*pos, 1 - core)

    def remote(src, dst, send, recv, dev):
        return pltpu.make_async_remote_copy(
            src_ref=src, dst_ref=dst, send_sem=send, recv_sem=recv, device_id=dev, device_id_type=MESH)

    barrier = pltpu.get_barrier_semaphore()
    everyone = [dev for dev, _ in group_peers] + slice_peers + [sibling]
    for dev in everyone:
        pl.semaphore_signal(barrier, inc=1, device_id=dev, device_id_type=MESH)
    load = pltpu.make_async_copy(b_ref, raw, loc_sem.at[0])
    load.start()
    kslot = kb.at[half[2], half[0], code]
    for o in range(2):
        for k in range(LOC):
            kslot[o * LOC + k:o * LOC + k + 1, :] = jnp.full((1, 128), keep_ref[o, k].astype(F32))

    load.wait()

    def turn(m, _):
        for p in range(0, PB, 32):
            part = raw[p:p + 32, pl.ds(pl.multiple_of(m * 16, 16), 16), :].astype(F32)
            part = jnp.swapaxes(part, 0, 1).astype(BF16)
            for i in range(16):
                b3[m * 8 + i // 2, p:p + 32, i % 2 * 256:i % 2 * 256 + 256] = part[i]
        return 0

    lax.fori_loop(0, 4, turn, 0)
    pl.semaphore_wait(barrier, len(everyone))

    first = code * OWN - HALO + NB

    def send_in(t):
        for dev, q in group_peers:
            batch = lax.rem(q * OWN - HALO + NB + t, NB)
            remote(b3.at[batch], bg.at[t, pl.ds(pl.multiple_of(code * PB, PB), PB)], a_send.at[0], a_recv.at[t], dev).start()

    for dev, q in group_peers:
        remote(kslot, kslot, k_send.at[0], k_recv.at[0], dev).start()
    for t in arrivals:
        send_in(t)

    def own_rows(t, _):
        batch = lax.rem(first + t, NB)
        bg[t, pl.ds(pl.multiple_of(code * PB, PB), PB), :] = b3[batch]
        return 0

    lax.fori_loop(0, LOC, own_rows, 0)

    for t in range(LOC):
        for o in range(2):
            orb = lax.rem(first + t, NB) * 2 + o
            for k in range(2):
                row = evir_ref[dom_ref[k, orb]] - eocc_ref[orb]
                lane = t * W + o * 256 + k * 128
                erow[:, lane:lane + 128] = row
                if t >= HALO:
                    at = lane - HALO * W
                    ecol[at:at + 128, :] = jnp.broadcast_to(row, (128, 128)).T

    def keep_group():
        pltpu.make_async_copy(kb.at[0, 0, pl.ds(0, 7)], kb.at[0, 0, pl.ds(0, 7)], k_recv.at[0]).wait()
        pltpu.make_async_copy(kb.at[0, 0, pl.ds(0, 7)], kb.at[0, 0, pl.ds(0, 7)], k_send.at[0]).wait()

    def keep_x():
        ref = kb.at[half[2], half[0]]
        return remote(ref, ref, k_send.at[1], k_recv.at[1], slice_peers[0])

    def keep_z():
        ref = kb.at[half[2]]
        return remote(ref, ref, k_send.at[2], k_recv.at[2], slice_peers[2])

    def order(u, n, h):
        return (u + n + h) % 3

    def cols(h):
        return pl.ds(h * 256, 256)

    def wait_in(t):
        pltpu.make_async_copy(bg.at[0, pl.ds(0, 7 * PB)], bg.at[0, pl.ds(0, 7 * PB)], a_recv.at[t]).wait()

    arrived, turned, touched = set(), set(), set()
    started = []
    left = [0] * LOC
    for top, s in units:
        left[top] += 1
        if s:
            left[top - s] += 1

    def core_copy(u):
        return remote(s0.at[started.index(u) % SLOTS], r0.at[u], c_send.at[u], c_recv.at[u], sibling)

    rs_bufs = ((s1, r1), (s2, r2), (s3, r3))

    def rs_copy(n, u, h):
        sb, rb = rs_bufs[n]
        return remote(sb.at[u, :, cols(h)], rb.at[u, :, cols(h)], rs_send.at[n, u, h], rs_recv.at[n, u, h],
                      slice_peers[order(u, n, h)])

    def base_rows(u, n, h):
        at = core * 0
        for m in range(n):
            at = at + half[order(u, m, h)] * (128 >> m)
        return at

    def ag_copy(n, u, h):
        size = 128 >> n
        ref = mb.at[u, pl.ds(pl.multiple_of(core * 256 + base_rows(u, n + 1, h), 32), size), cols(h)]
        return remote(ref, ref, ag_send.at[n, u, h], ag_recv.at[n, u, h], slice_peers[order(u, n, h)])

    def gc_copy(u):
        ref = mb.at[u, pl.ds(pl.multiple_of(core * 256, 256), 256)]
        return remote(ref, ref, gc_send.at[u], gc_recv.at[u], sibling)

    def stage_v(u):
        top, s = units[u]
        for t in (top, top - s):
            if t not in arrived:
                wait_in(t)
                arrived.add(t)
        own = top - HALO
        if top not in turned:
            turned.add(top)
            for h in range(2):
                lanes = core * 256 if h == 0 else (1 - core) * 256
                bt[own, h] = bg[top, :, pl.ds(pl.multiple_of(lanes, 256), 256)].T
        if len(started) >= SLOTS:
            core_copy(started[-SLOTS]).wait_send()
        started.append(u)
        other = bg[top - s]
        s0[started.index(u) % SLOTS] = jnp.dot(bt[own, 1], other, preferred_element_type=F32)
        core_copy(u).start()
        acc[u] = jnp.dot(bt[own, 0], other, preferred_element_type=F32)

    def fold(n, u):
        src = r0 if n == 0 else rs_bufs[n - 1][1]
        size = 128 >> n
        send_to = rs_bufs[n][0]
        step = 32
        if n == 0:
            core_copy(u).wait_recv()
        for h in range(2):
            if n:
                rs_copy(n - 1, u, h).wait_recv()
            lanes = slice(h * 256, h * 256 + 256)
            base = base_rows(u, n, h)
            send_at = (1 - half[order(u, n, h)]) * size

            def far(k, _):
                near = pl.ds(pl.multiple_of(send_at + k * step, step), step)
                mine = pl.ds(pl.multiple_of(base + send_at + k * step, step), step)
                val = acc[u, mine, lanes] + src[u, near, lanes].astype(F32)
                send_to[u, pl.ds(pl.multiple_of(k * step, step), step), lanes] = val.astype(send_to.dtype)
                return 0

            lax.fori_loop(0, size // step, far, 0)
            rs_copy(n, u, h).start()
        for h in range(2):
            lanes = slice(h * 256, h * 256 + 256)
            base = base_rows(u, n, h)
            keep_at = half[order(u, n, h)] * size

            def stay(k, _):
                near = pl.ds(pl.multiple_of(keep_at + k * step, step), step)
                mine = pl.ds(pl.multiple_of(base + keep_at + k * step, step), step)
                acc[u, mine, lanes] = acc[u, mine, lanes] + src[u, near, lanes].astype(F32)
                return 0

            lax.fori_loop(0, size // step, stay, 0)

    def stage_amp(u):
        top, s = units[u]
        for h in range(2):
            rs_copy(2, u, h).wait_recv()
            base = pl.multiple_of(base_rows(u, 3, h), 32)
            rows = ecol[pl.ds(pl.multiple_of((top - HALO) * W + core * 256 + base, 32), 32), :]
            for k in range(2 * h, 2 * h + 2):
                lanes = slice(k * 128, k * 128 + 128)
                at = (top - s) * W + k * 128
                total = acc[u, pl.ds(base, 32), lanes] + r3[u, :, lanes].astype(F32)
                denom = rows + erow[:, at:at + 128]
                mb[u, pl.ds(pl.multiple_of(core * 256 + base, 32), 32), lanes] = (-total / denom).astype(BF16)
            ag_copy(2, u, h).start()

    def stage_ag(n, u):
        for h in range(2):
            ag_copy(n + 1, u, h).wait_recv()
            ag_copy(n, u, h).start()

    def stage_gc(u):
        for h in range(2):
            ag_copy(0, u, h).wait_recv()
        gc_copy(u).start()

    def flag(t, orbital, offset):
        batch = lax.rem(first + t, NB)
        y = half[1] * 2 + lax.rem(lax.div(batch, 4), 2)
        x, z = lax.div(batch, 8), lax.rem(batch, 4)
        q = side(x) * 4 + side(y) * 2 + side(z)
        row = orbital * LOC + offset
        line = kb[lax.div(z, 2), lax.div(x, 2), q, row:row + 1, :]
        return jnp.broadcast_to(line, (256, 128)).astype(BF16)

    finished = []

    def finish(t):
        finished.append(t)
        go[t] = gam[t].astype(BF16)
        for dev, q in group_peers:
            remote(go.at[t, pl.ds(pl.multiple_of(q * PB, PB), PB)], rr.at[code, t], o_send.at[0], o_recv.at[t], dev).start()
        rr[code, t] = go[t, pl.ds(pl.multiple_of(code * PB, PB), PB)]

    def add_term(t, part):
        if t in touched:
            gam[t] = gam[t] + part
        else:
            touched.add(t)
            gam[t] = part
        left[t] -= 1
        if left[t] == 0:
            finish(t)

    def stage_gamma(u):
        top, s = units[u]
        gc_copy(u).wait_recv()
        if s:
            for o in range(2):
                m = flag(top - s, o, HALO - s)
                for k in range(2):
                    lanes = slice(o * 256 + k * 128, o * 256 + k * 128 + 128)
                    for h in range(2):
                        mm[0, h * 256:h * 256 + 256, lanes] = mb[u, h * 256:h * 256 + 256, lanes] * m
            add_term(top - s, jnp.dot(bg[top], mm[0], preferred_element_type=F32))
        for h in range(2):
            m = flag(top, h, HALO + s)
            for k in range(4):
                lanes = slice(k * 128, k * 128 + 128)
                mm[1, h * 256:h * 256 + 256, lanes] = mb[u, h * 256:h * 256 + 256, lanes] * m
        add_term(top, lax.dot_general(bg[top - s], mm[1], (((1,), (1,)), ((), ())), preferred_element_type=F32))

    stages = [
        stage_v,
        lambda u: fold(0, u),
        lambda u: fold(1, u),
        lambda u: fold(2, u),
        stage_amp,
        lambda u: stage_ag(1, u),
        lambda u: stage_ag(0, u),
        stage_gc,
        stage_gamma,
    ]
    seen = set()
    for stage, u in steps:
        if stage not in seen:
            if stage == 1:
                keep_group()
                keep_x().start()
            if stage == 4:
                keep_x().wait()
                keep_z().start()
            if stage == 8:
                keep_z().wait()
        seen.add(stage)
        stages[stage](u)

    pltpu.make_async_copy(rr.at[pl.ds(0, 7)], rr.at[pl.ds(0, 7)], a_send.at[0]).wait()
    for at, u in enumerate(started):
        if at >= len(started) - SLOTS:
            core_copy(u).wait_send()
        gc_copy(u).wait_send()
        for n in range(3):
            for h in range(2):
                rs_copy(n, u, h).wait_send()
                ag_copy(n, u, h).wait_send()

    got, done = set(), set()
    stores = []
    for t in finished:
        pltpu.make_async_copy(bg.at[0, pl.ds(0, 7 * PB)], bg.at[0, pl.ds(0, 7 * PB)], o_recv.at[t]).wait()
        got.add(t)
        for k in range(OWN):
            if k in done or HALO + k not in got or (k and k - 1 not in got):
                continue
            done.add(k)
            if k:
                def combine(g, _, k=k):
                    nxt = lax.rem(g + 1, NCODE)
                    rr[g, HALO + k] = (rr[g, HALO + k].astype(F32) + rr[nxt, k - 1].astype(F32)).astype(BF16)
                    return 0

                lax.fori_loop(0, NCODE, combine, 0)

    for m in range(4):
        for p in range(0, PB, 32):
            part = jnp.stack([rr[m * 2 + i // 8, HALO + i // 2 % 4, p:p + 32, i % 2 * 256:i % 2 * 256 + 256] for i in range(16)])
            raw[p:p + 32, m * 16:m * 16 + 16, :] = jnp.swapaxes(part.astype(F32), 0, 1).astype(BF16)
        cp = pltpu.make_async_copy(raw.at[:, pl.ds(m * 16, 16)], out_ref.at[:, pl.ds(m * 16, 16)], out_sem.at[m, 0])
        cp.start()
        stores.append(cp)
    for cp in stores:
        cp.wait()
    pltpu.make_async_copy(rr.at[pl.ds(0, 7)], rr.at[pl.ds(0, 7)], o_send.at[0]).wait()


def shards(b_aux, eps_occ, eps_vir, domains, pair_keep):
    dma, vm = pltpu.SemaphoreType.DMA, pltpu.VMEM
    hbm = pl.BlockSpec(memory_space=pl.ANY)
    vmem = pl.BlockSpec(memory_space=pltpu.VMEM)
    smem = pl.BlockSpec(memory_space=pltpu.SMEM)
    rs1, rs2, rs3 = RS_DTYPES
    n = len(UNITS)
    return pl.pallas_call(
        functools.partial(kernel, STEPS, ARRIVALS, UNITS),
        out_shape=jax.ShapeDtypeStruct((PB, 2 * NB, 256), BF16),
        in_specs=[hbm, vmem, smem, smem, smem],
        out_specs=hbm,
        scratch_shapes=[
            vm((PB, 2 * NB, 256), BF16),
            vm((NB, PB, W), BF16),
            vm((LOC, PS, W), BF16),
            vm((OWN, 2, 256, PS), BF16),
            vm((n, 256, W), F32),
            vm((SLOTS, 256, W), F32), vm((n, 256, W), F32),
            vm((n, 128, W), rs1), vm((n, 128, W), rs1),
            vm((n, 64, W), rs2), vm((n, 64, W), rs2),
            vm((n, 32, W), rs3), vm((n, 32, W), rs3),
            vm((n, W, W), BF16),
            vm((2, W, W), BF16),
            vm((LOC, PS, W), F32),
            vm((LOC, PS, W), BF16),
            vm((NCODE, LOC, PB, W), BF16),
            vm((2, 2, NCODE, 16, 128), F32),
            vm((1, LOC * W), F32),
            vm((OWN * W, 128), F32),
            dma((2,)), dma((OWN, 2)), dma((1,)), dma((LOC,)),
            dma((n,)), dma((n,)),
            dma((3, n, 2)), dma((3, n, 2)),
            dma((3, n, 2)), dma((3, n, 2)),
            dma((n,)), dma((n,)),
            dma((1,)), dma((LOC,)),
            dma((3,)), dma((3,)),
        ],
        compiler_params=pltpu.CompilerParams(
            collective_id=0, has_side_effects=True, vmem_limit_bytes=62 * 1024 * 1024),
    )(b_aux, eps_vir.reshape(32, 1, 128), eps_occ, domains.T, pair_keep)


def solution(mesh):
    in_specs = (P(("occ", "aux"), None, None), P(), P(), P(), P("occ", None))
    out_specs = P(("occ", "aux"), None, None)
    return jax.shard_map(shards, mesh=mesh, in_specs=in_specs, out_specs=out_specs, check_vma=False)
```

```python
import functools

import jax
import jax.numpy as jnp
from jax import lax
from jax.experimental import pallas as pl
from jax.experimental.pallas import tpu as pltpu
from jax.sharding import PartitionSpec as P

MESH = pl.DeviceIdType.MESH
F32 = jnp.float32
BF16 = jnp.bfloat16

PB = 64
W = 512
NB = 32
OWN = 4
HALO = 3
LOC = OWN + HALO
NCODE = 8
PS = NCODE * PB
SLOTS = 4
ARRIVALS = (3, 1, 4, 0, 6, 5, 2)
UNITS = (
    (6, 1), (6, 2), (3, 0), (4, 2), (4, 3), (3, 2), (4, 0), (5, 1),
    (6, 3), (5, 3), (6, 0), (3, 1), (4, 1), (3, 3), (5, 2), (5, 0),
)
STEPS = (
    (0, 2), (1, 2), (0, 5), (2, 2), (1, 5), (0, 4), (3, 2), (0, 6), (0, 12), (2, 5), (1, 4), (1, 6),
    (1, 12), (4, 2), (0, 13), (3, 5), (1, 13), (2, 4), (2, 6), (2, 12), (5, 2), (4, 5), (0, 1), (0, 8),
    (0, 10), (2, 13), (1, 1), (3, 4), (1, 8), (3, 6), (1, 10), (3, 12), (6, 2), (5, 5), (0, 0), (3, 13),
    (0, 7), (4, 4), (2, 1), (1, 0), (1, 7), (2, 8), (4, 6), (6, 5), (2, 10), (4, 12), (4, 13), (5, 4),
    (7, 2), (0, 3), (3, 1), (2, 0), (8, 2), (1, 3), (2, 7), (5, 6), (3, 8), (7, 5), (0, 9), (3, 10),
    (6, 4), (5, 12), (5, 13), (8, 5), (3, 0), (4, 1), (1, 9), (2, 3), (6, 6), (3, 7), (4, 8), (4, 10),
    (7, 4), (0, 11), (6, 12), (5, 1), (6, 13), (8, 4), (4, 0), (1, 11), (2, 9), (3, 3), (7, 6), (0, 14),
    (4, 7), (5, 8), (5, 10), (8, 6), (5, 0), (6, 1), (1, 14), (7, 12), (0, 15), (2, 11), (8, 12), (4, 3),
    (3, 9), (7, 13), (1, 15), (5, 7), (6, 10), (6, 8), (8, 13), (6, 0), (7, 1), (3, 11), (2, 14), (5, 3),
    (8, 1), (4, 9), (2, 15), (6, 7), (7, 10), (8, 10), (7, 0), (7, 8), (4, 11), (3, 14), (5, 9), (6, 3),
    (8, 0), (3, 15), (8, 8), (7, 7), (5, 11), (4, 14), (6, 9), (8, 7), (4, 15), (7, 3), (6, 11), (8, 3),
    (5, 14), (7, 9), (5, 15), (8, 9), (7, 11), (6, 14), (8, 11), (6, 15), (7, 14), (8, 14), (7, 15), (8, 15),
)
RS_DTYPES = (BF16, BF16, BF16)


def side(pos):
    return lax.rem(lax.div(pos + 1, 2), 2)


def kernel(steps, arrivals, units, b_ref, evir_ref, eocc_ref, dom_ref, keep_ref, out_ref,
           raw, b3, bg, bt, acc, s0, r0, s1, r1, s2, r2, s3, r3, mb, mm, gam, go, rr, kb, erow, ecol,
           loc_sem, out_sem, a_send, a_recv, c_send, c_recv, rs_send, rs_recv, ag_send, ag_recv,
           gc_send, gc_recv, o_send, o_recv, k_send, k_recv):
    occ = lax.axis_index("occ")
    aux = lax.axis_index("aux")
    core = lax.rem(aux, 2)
    pos = (lax.div(occ, 8), lax.div(aux, 2) * 2 + lax.rem(lax.div(occ, 4), 2), lax.rem(occ, 4))
    half = tuple(lax.div(p, 2) for p in pos)
    fs = tuple(side(p) for p in pos)
    code = fs[0] * 4 + fs[1] * 2 + fs[2]

    def device(x, y, z, c):
        return (x * 8 + lax.rem(y, 2) * 4 + z, lax.div(y, 2) * 2 + c)

    group_peers = []
    for r in range(1, 8):
        bits = ((r >> 2) & 1, (r >> 1) & 1, r & 1)
        where = [p + 1 - 2 * lax.rem(p, 2) if bit else p for p, bit in zip(pos, bits)]
        flips = [1 - f if bit else f for f, bit in zip(fs, bits)]
        group_peers.append((device(*where, core), flips[0] * 4 + flips[1] * 2 + flips[2]))
    slice_peers = []
    for d in range(3):
        where = list(pos)
        where[d] = 3 - pos[d]
        slice_peers.append(device(*where, core))
    sibling = device(*pos, 1 - core)

    def remote(src, dst, send, recv, dev):
        return pltpu.make_async_remote_copy(
            src_ref=src, dst_ref=dst, send_sem=send, recv_sem=recv, device_id=dev, device_id_type=MESH)

    barrier = pltpu.get_barrier_semaphore()
    everyone = [dev for dev, _ in group_peers] + slice_peers + [sibling]
    for dev in everyone:
        pl.semaphore_signal(barrier, inc=1, device_id=dev, device_id_type=MESH)
    load = pltpu.make_async_copy(b_ref, raw, loc_sem.at[0])
    load.start()
    kslot = kb.at[half[2], half[0], code]
    for o in range(2):
        for k in range(LOC):
            kslot[o * LOC + k:o * LOC + k + 1, :] = jnp.full((1, 128), keep_ref[o, k].astype(F32))

    load.wait()

    def turn(m, _):
        for p in range(0, PB, 32):
            part = raw[p:p + 32, pl.ds(pl.multiple_of(m * 16, 16), 16), :].astype(F32)
            part = jnp.swapaxes(part, 0, 1).astype(BF16)
            for i in range(16):
                b3[m * 8 + i // 2, p:p + 32, i % 2 * 256:i % 2 * 256 + 256] = part[i]
        return 0

    lax.fori_loop(0, 4, turn, 0)
    pl.semaphore_wait(barrier, len(everyone))

    first = code * OWN - HALO + NB

    def send_in(t):
        for dev, q in group_peers:
            batch = lax.rem(q * OWN - HALO + NB + t, NB)
            remote(b3.at[batch], bg.at[t, pl.ds(pl.multiple_of(code * PB, PB), PB)], a_send.at[0], a_recv.at[t], dev).start()

    for dev, q in group_peers:
        remote(kslot, kslot, k_send.at[0], k_recv.at[0], dev).start()
    for t in arrivals:
        send_in(t)

    def own_rows(t, _):
        batch = lax.rem(first + t, NB)
        bg[t, pl.ds(pl.multiple_of(code * PB, PB), PB), :] = b3[batch]
        return 0

    lax.fori_loop(0, LOC, own_rows, 0)

    for t in range(LOC):
        for o in range(2):
            orb = lax.rem(first + t, NB) * 2 + o
            for k in range(2):
                row = evir_ref[dom_ref[k, orb]] - eocc_ref[orb]
                lane = t * W + o * 256 + k * 128
                erow[:, lane:lane + 128] = row
                if t >= HALO:
                    at = lane - HALO * W
                    ecol[at:at + 128, :] = jnp.broadcast_to(row, (128, 128)).T

    def keep_group():
        pltpu.make_async_copy(kb.at[0, 0, pl.ds(0, 7)], kb.at[0, 0, pl.ds(0, 7)], k_recv.at[0]).wait()
        pltpu.make_async_copy(kb.at[0, 0, pl.ds(0, 7)], kb.at[0, 0, pl.ds(0, 7)], k_send.at[0]).wait()

    def keep_x():
        ref = kb.at[half[2], half[0]]
        return remote(ref, ref, k_send.at[1], k_recv.at[1], slice_peers[0])

    def keep_z():
        ref = kb.at[half[2]]
        return remote(ref, ref, k_send.at[2], k_recv.at[2], slice_peers[2])

    def order(u, n, h):
        return (u + n + h) % 3

    def cols(h):
        return pl.ds(h * 256, 256)

    def wait_in(t):
        pltpu.make_async_copy(bg.at[0, pl.ds(0, 7 * PB)], bg.at[0, pl.ds(0, 7 * PB)], a_recv.at[t]).wait()

    arrived, turned, touched = set(), set(), set()
    started = []
    left = [0] * LOC
    for top, s in units:
        left[top] += 1
        if s:
            left[top - s] += 1

    def core_copy(u):
        return remote(s0.at[started.index(u) % SLOTS], r0.at[u], c_send.at[u], c_recv.at[u], sibling)

    rs_bufs = ((s1, r1), (s2, r2), (s3, r3))

    def rs_copy(n, u, h):
        sb, rb = rs_bufs[n]
        return remote(sb.at[u, :, cols(h)], rb.at[u, :, cols(h)], rs_send.at[n, u, h], rs_recv.at[n, u, h],
                      slice_peers[order(u, n, h)])

    def base_rows(u, n, h):
        at = core * 0
        for m in range(n):
            at = at + half[order(u, m, h)] * (128 >> m)
        return at

    def ag_copy(n, u, h):
        size = 128 >> n
        ref = mb.at[u, pl.ds(pl.multiple_of(core * 256 + base_rows(u, n + 1, h), 32), size), cols(h)]
        return remote(ref, ref, ag_send.at[n, u, h], ag_recv.at[n, u, h], slice_peers[order(u, n, h)])

    def ag_piece(n, u, h, at, size):
        ref = mb.at[u, pl.ds(pl.multiple_of(core * 256 + at, 32), size), cols(h)]
        remote(ref, ref, ag_send.at[n, u, h], ag_recv.at[n, u, h], slice_peers[order(u, n, h)]).start()

    def gc_copy(u):
        ref = mb.at[u, pl.ds(pl.multiple_of(core * 256, 256), 256)]
        return remote(ref, ref, gc_send.at[u], gc_recv.at[u], sibling)

    def stage_v(u):
        top, s = units[u]
        for t in (top, top - s):
            if t not in arrived:
                wait_in(t)
                arrived.add(t)
        own = top - HALO
        if top not in turned:
            turned.add(top)
            for h in range(2):
                lanes = core * 256 if h == 0 else (1 - core) * 256
                bt[own, h] = bg[top, :, pl.ds(pl.multiple_of(lanes, 256), 256)].T
        if len(started) >= SLOTS:
            core_copy(started[-SLOTS]).wait_send()
        started.append(u)
        other = bg[top - s]
        s0[started.index(u) % SLOTS] = jnp.dot(bt[own, 1], other, preferred_element_type=F32)
        core_copy(u).start()
        acc[u] = jnp.dot(bt[own, 0], other, preferred_element_type=F32)

    def fold(n, u):
        src = r0 if n == 0 else rs_bufs[n - 1][1]
        size = 128 >> n
        send_to = rs_bufs[n][0]
        step = 32
        if n == 0:
            core_copy(u).wait_recv()
        for h in range(2):
            if n:
                rs_copy(n - 1, u, h).wait_recv()
            lanes = slice(h * 256, h * 256 + 256)
            base = base_rows(u, n, h)
            send_at = (1 - half[order(u, n, h)]) * size

            def far(k, _):
                near = pl.ds(pl.multiple_of(send_at + k * step, step), step)
                mine = pl.ds(pl.multiple_of(base + send_at + k * step, step), step)
                val = acc[u, mine, lanes] + src[u, near, lanes].astype(F32)
                send_to[u, pl.ds(pl.multiple_of(k * step, step), step), lanes] = val.astype(send_to.dtype)
                return 0

            lax.fori_loop(0, size // step, far, 0)
            rs_copy(n, u, h).start()
        for h in range(2):
            lanes = slice(h * 256, h * 256 + 256)
            base = base_rows(u, n, h)
            keep_at = half[order(u, n, h)] * size

            def stay(k, _):
                near = pl.ds(pl.multiple_of(keep_at + k * step, step), step)
                mine = pl.ds(pl.multiple_of(base + keep_at + k * step, step), step)
                acc[u, mine, lanes] = acc[u, mine, lanes] + src[u, near, lanes].astype(F32)
                return 0

            lax.fori_loop(0, size // step, stay, 0)

    def stage_amp(u):
        top, s = units[u]
        for h in range(2):
            rs_copy(2, u, h).wait_recv()
            base = pl.multiple_of(base_rows(u, 3, h), 32)
            rows = ecol[pl.ds(pl.multiple_of((top - HALO) * W + core * 256 + base, 32), 32), :]
            for k in range(2 * h, 2 * h + 2):
                lanes = slice(k * 128, k * 128 + 128)
                at = (top - s) * W + k * 128
                total = acc[u, pl.ds(base, 32), lanes] + r3[u, :, lanes].astype(F32)
                denom = rows + erow[:, at:at + 128]
                mb[u, pl.ds(pl.multiple_of(core * 256 + base, 32), 32), lanes] = (-total / denom).astype(BF16)
            for n in (2, 1, 0):
                ag_piece(n, u, h, base_rows(u, 3, h), 32)

    def stage_ag(n, u):
        for h in range(2):
            ag_copy(n + 1, u, h).wait_recv()
            size = 64 >> n
            at = base_rows(u, n + 1, h) + (1 - half[order(u, n + 1, h)]) * size
            for m in range(n, -1, -1):
                ag_piece(m, u, h, at, size)

    def stage_gc(u):
        for h in range(2):
            ag_copy(0, u, h).wait_recv()
        gc_copy(u).start()

    def flag(t, orbital, offset):
        batch = lax.rem(first + t, NB)
        y = half[1] * 2 + lax.rem(lax.div(batch, 4), 2)
        x, z = lax.div(batch, 8), lax.rem(batch, 4)
        q = side(x) * 4 + side(y) * 2 + side(z)
        row = orbital * LOC + offset
        line = kb[lax.div(z, 2), lax.div(x, 2), q, row:row + 1, :]
        return jnp.broadcast_to(line, (256, 128)).astype(BF16)

    finished = []

    def finish(t):
        finished.append(t)
        go[t] = gam[t].astype(BF16)
        for dev, q in group_peers:
            remote(go.at[t, pl.ds(pl.multiple_of(q * PB, PB), PB)], rr.at[code, t], o_send.at[0], o_recv.at[t], dev).start()
        rr[code, t] = go[t, pl.ds(pl.multiple_of(code * PB, PB), PB)]

    def add_term(t, part):
        if t in touched:
            gam[t] = gam[t] + part
        else:
            touched.add(t)
            gam[t] = part
        left[t] -= 1
        if left[t] == 0:
            finish(t)

    def stage_gamma(u):
        top, s = units[u]
        gc_copy(u).wait_recv()
        if s:
            for o in range(2):
                m = flag(top - s, o, HALO - s)
                for k in range(2):
                    lanes = slice(o * 256 + k * 128, o * 256 + k * 128 + 128)
                    for h in range(2):
                        mm[0, h * 256:h * 256 + 256, lanes] = mb[u, h * 256:h * 256 + 256, lanes] * m
            add_term(top - s, jnp.dot(bg[top], mm[0], preferred_element_type=F32))
        for h in range(2):
            m = flag(top, h, HALO + s)
            for k in range(4):
                lanes = slice(k * 128, k * 128 + 128)
                mm[1, h * 256:h * 256 + 256, lanes] = mb[u, h * 256:h * 256 + 256, lanes] * m
        add_term(top, lax.dot_general(bg[top - s], mm[1], (((1,), (1,)), ((), ())), preferred_element_type=F32))

    stages = [
        stage_v,
        lambda u: fold(0, u),
        lambda u: fold(1, u),
        lambda u: fold(2, u),
        stage_amp,
        lambda u: stage_ag(1, u),
        lambda u: stage_ag(0, u),
        stage_gc,
        stage_gamma,
    ]
    seen = set()
    for stage, u in steps:
        if stage not in seen:
            if stage == 1:
                keep_group()
                keep_x().start()
            if stage == 4:
                keep_x().wait()
                keep_z().start()
            if stage == 8:
                keep_z().wait()
        seen.add(stage)
        stages[stage](u)

    pltpu.make_async_copy(rr.at[pl.ds(0, 7)], rr.at[pl.ds(0, 7)], a_send.at[0]).wait()
    for at, u in enumerate(started):
        if at >= len(started) - SLOTS:
            core_copy(u).wait_send()
        gc_copy(u).wait_send()
        for n in range(3):
            for h in range(2):
                rs_copy(n, u, h).wait_send()
                ag_copy(n, u, h).wait_send()

    got, done = set(), set()
    stores = []
    for t in finished:
        pltpu.make_async_copy(bg.at[0, pl.ds(0, 7 * PB)], bg.at[0, pl.ds(0, 7 * PB)], o_recv.at[t]).wait()
        got.add(t)
        for k in range(OWN):
            if k in done or HALO + k not in got or (k and k - 1 not in got):
                continue
            done.add(k)
            if k:
                def combine(g, _, k=k):
                    nxt = lax.rem(g + 1, NCODE)
                    rr[g, HALO + k] = (rr[g, HALO + k].astype(F32) + rr[nxt, k - 1].astype(F32)).astype(BF16)
                    return 0

                lax.fori_loop(0, NCODE, combine, 0)

    for m in range(4):
        for p in range(0, PB, 32):
            part = jnp.stack([rr[m * 2 + i // 8, HALO + i // 2 % 4, p:p + 32, i % 2 * 256:i % 2 * 256 + 256] for i in range(16)])
            raw[p:p + 32, m * 16:m * 16 + 16, :] = jnp.swapaxes(part.astype(F32), 0, 1).astype(BF16)
        cp = pltpu.make_async_copy(raw.at[:, pl.ds(m * 16, 16)], out_ref.at[:, pl.ds(m * 16, 16)], out_sem.at[m, 0])
        cp.start()
        stores.append(cp)
    for cp in stores:
        cp.wait()
    pltpu.make_async_copy(rr.at[pl.ds(0, 7)], rr.at[pl.ds(0, 7)], o_send.at[0]).wait()


def shards(b_aux, eps_occ, eps_vir, domains, pair_keep):
    dma, vm = pltpu.SemaphoreType.DMA, pltpu.VMEM
    hbm = pl.BlockSpec(memory_space=pl.ANY)
    vmem = pl.BlockSpec(memory_space=pltpu.VMEM)
    smem = pl.BlockSpec(memory_space=pltpu.SMEM)
    rs1, rs2, rs3 = RS_DTYPES
    n = len(UNITS)
    return pl.pallas_call(
        functools.partial(kernel, STEPS, ARRIVALS, UNITS),
        out_shape=jax.ShapeDtypeStruct((PB, 2 * NB, 256), BF16),
        in_specs=[hbm, vmem, smem, smem, smem],
        out_specs=hbm,
        scratch_shapes=[
            vm((PB, 2 * NB, 256), BF16),
            vm((NB, PB, W), BF16),
            vm((LOC, PS, W), BF16),
            vm((OWN, 2, 256, PS), BF16),
            vm((n, 256, W), F32),
            vm((SLOTS, 256, W), F32), vm((n, 256, W), F32),
            vm((n, 128, W), rs1), vm((n, 128, W), rs1),
            vm((n, 64, W), rs2), vm((n, 64, W), rs2),
            vm((n, 32, W), rs3), vm((n, 32, W), rs3),
            vm((n, W, W), BF16),
            vm((2, W, W), BF16),
            vm((LOC, PS, W), F32),
            vm((LOC, PS, W), BF16),
            vm((NCODE, LOC, PB, W), BF16),
            vm((2, 2, NCODE, 16, 128), F32),
            vm((1, LOC * W), F32),
            vm((OWN * W, 128), F32),
            dma((2,)), dma((OWN, 2)), dma((1,)), dma((LOC,)),
            dma((n,)), dma((n,)),
            dma((3, n, 2)), dma((3, n, 2)),
            dma((3, n, 2)), dma((3, n, 2)),
            dma((n,)), dma((n,)),
            dma((1,)), dma((LOC,)),
            dma((3,)), dma((3,)),
        ],
        compiler_params=pltpu.CompilerParams(
            collective_id=0, has_side_effects=True, vmem_limit_bytes=62 * 1024 * 1024),
    )(b_aux, eps_vir.reshape(32, 1, 128), eps_occ, domains.T, pair_keep)


def solution(mesh):
    in_specs = (P(("occ", "aux"), None, None), P(), P(), P(), P("occ", None))
    out_specs = P(("occ", "aux"), None, None)
    return jax.shard_map(shards, mesh=mesh, in_specs=in_specs, out_specs=out_specs, check_vma=False)
```
